128 devices in a mesh: group: 4 (over y), ingroup: 32 (over x, z, core).
Axes of the slice: x: 4, y: 4, z: 4, core: 2. Of those that a mesh axis runs over, the one named last changes fastest.
Arguments:
- tokens: bfloat16 [16384, 2048], P(('group', 'ingroup')), may hold values from -6 to 6
- cotangent: bfloat16 [16384, 2048], P(('group', 'ingroup')), may hold values from -6 to 6
- routes: int32 [16384, 8], P(('group', 'ingroup')), may hold values from 0 to 127, all different within a row; in each aligned block of 128 rows (0 to 127, 128 to 255, ...) at most 10 rows name the same one
- gate_weights: float32 [16384, 8], P(('group', 'ingroup')), may hold values from 0.1 to 1
- weight_gate: bfloat16 [128, 2048, 768], P(('group', 'ingroup')), may hold values from -0.125 to 0.125
- weight_up: bfloat16 [128, 2048, 768], P(('group', 'ingroup')), may hold values from -0.125 to 0.125
- weight_down: bfloat16 [128, 768, 2048], P(('group', 'ingroup')), may hold values from -0.21875 to 0.21875
Outputs:
- mixed: bfloat16 [16384, 2048], P(('group', 'ingroup'))
- grad_tokens: bfloat16 [16384, 2048], P(('group', 'ingroup'))
- grad_gates: float32 [16384, 8], P(('group', 'ingroup'))
- grad_weight_gate: bfloat16 [128, 2048, 768], P(('group', 'ingroup'))
- grad_weight_up: bfloat16 [128, 2048, 768], P(('group', 'ingroup'))
- grad_weight_down: bfloat16 [128, 768, 2048], P(('group', 'ingroup'))
The draws below stay inside these ranges and needn't reach their ends.
Inputs may be any that keep to these rules, and one draw needn't show every extreme that they name: `routes`: each row names 8 different experts. Among the rows of one device no expert is named more than 10 times, and in every draw some expert is named exactly 10 times by the rows of some device.
All inputs are finite; a program needn't handle non-finite values.
Results may differ from the reference program's by a relative error of at most 0.015.
Values may be sent and summed in bfloat16 or wider, within the bound.
A program may use at most 192 MiB of HBM per device.

```python
import math
import jax
import jax.numpy as jnp
import numpy as np
from jax import lax

D = 2048
FF = 768
TOP = 8
TOK_DEV = 128
EXPERTS = 128
TOKENS = 16384
CAP = 10


def block_scale(own_key, dims, cuts, smallest, largest):
    gain = 1.0
    for dim, shards_of in cuts:
        draws = jax.random.uniform(jax.random.fold_in(jax.random.fold_in(own_key, 6), dim), (shards_of,), jnp.float32, smallest / len(cuts), largest / len(cuts))
        gain = gain * jnp.repeat(jnp.exp(draws), dims[dim] // shards_of).reshape((-1,) + (1,) * (len(dims) - 1 - dim))
    return gain


def assign_block(key, own, number, rows, count, top, reach, lean):
    ranking = jax.random.permutation(key, count)
    heavy_load, ordinary = load_shares(count, rows * top, reach, lean, True), load_shares(count, rows * top, reach, lean, False)
    places = jnp.arange(count)

    def named(tallies, offset_by):
        used = int((tallies > 0).sum())
        fixed = max(1, used // 4)
        shifted = fixed + (places - fixed + offset_by * (used - fixed)) % max(1, count - fixed)
        return jnp.zeros((count,), jnp.int32).at[ranking[jnp.where(places < fixed, places, shifted)]].set(jnp.asarray(tallies, jnp.int32))

    tallies = jnp.where(number % 4 == 0, named(heavy_load, number // 4), named(ordinary, number - number // 4 - 1))
    mixed = jax.random.permutation(jax.random.fold_in(own, 3), count)
    donor, sink = mixed[0:count // 2 * 2:2], mixed[1:count // 2 * 2:2]
    slack = jnp.minimum(tallies[donor] - 1, reach - tallies[sink]) // 2
    slack = jnp.where((donor == ranking[0]) | (sink == ranking[0]) | (tallies[sink] == 0), 0, jnp.maximum(slack, 0))
    shifted = jax.random.randint(jax.random.fold_in(own, 4), (count // 2,), 0, 1 << 20) % (slack + 1)
    tallies = tallies.at[donor].add(-shifted).at[sink].add(shifted)
    labels = jnp.searchsorted(jnp.cumsum(tallies), jnp.arange(rows * top), side="right").astype(jnp.int32)
    grid = labels.reshape(top, rows).T
    grid = grid[jax.random.permutation(jax.random.fold_in(own, 1), rows)]
    offset_by = jax.random.randint(jax.random.fold_in(own, 2), (rows, 1), 0, top)
    return jnp.take_along_axis(grid, (jnp.arange(top)[None, :] + offset_by) % top, axis=1)


def load_shares(count, total, most, lean, full):
    portions = [(1 << 20) // math.isqrt(grade ** lean) + 1 for grade in range(1, count + 1)]
    largest = most if full else min(most, max(-(-total // count), total * portions[0] // sum(portions)))
    least = 1 if total - largest >= count - 1 else 0
    holding, rest = [largest] + [least] * (count - 1), total - largest - least * (count - 1)
    while rest > 0:
        candidates = [i for i in range(1, count) if holding[i] < largest] or [i for i in range(1, count) if holding[i] < most]
        pool, left = sum([portions[i] for i in candidates]), rest
        for i in candidates:
            more = min(most - holding[i], max(1, left * portions[i] // pool), rest)
            holding[i] = holding[i] + more
            rest = rest - more
    return np.array(holding)


def centred(stream_key, dims, width, most, shards=(), held_as=jnp.bfloat16):
    array = width * jax.random.normal(stream_key, dims, jnp.float32)
    if shards:
        array = array * block_scale(stream_key, dims, shards, -0.22, 0.18)
    return jnp.clip(array, -most, most).astype(held_as)


def setup_inputs(seed: int = 0) -> dict:
    streams_of = jax.random.split(jax.random.key(seed), 8)
    tokens = centred(streams_of[0], (TOKENS, D), 1.0, 6.0, ((0, 128),))
    cotangent = centred(streams_of[1], (TOKENS, D), 1.0, 6.0, ((0, 128),))
    routes_keys = jax.random.split(jax.random.fold_in(streams_of[2], 1), TOKENS // TOK_DEV)
    routes_turns = jax.random.permutation(jax.random.fold_in(streams_of[2], 3), TOKENS // TOK_DEV)
    routes = jax.vmap(lambda own, number: assign_block(jax.random.fold_in(streams_of[2], 2), own, number, TOK_DEV, EXPERTS, TOP, CAP, 2))(routes_keys, routes_turns).reshape((TOKENS, TOP))
    gate_weights = jnp.clip(0.1 + 0.9 * jax.random.uniform(streams_of[3], (TOKENS, TOP), jnp.float32) ** block_scale(streams_of[3], (TOKENS, TOP), ((0, 128),), -0.2, 0.2), 0.1, 1.0)
    weight_gate = centred(streams_of[4], (EXPERTS, D, FF), D ** -0.5, 0.125, ((0, 128),))
    weight_up = centred(streams_of[5], (EXPERTS, D, FF), D ** -0.5, 0.125, ((0, 128),))
    weight_down = centred(streams_of[6], (EXPERTS, FF, D), FF ** -0.5, 0.21875, ((0, 128),))
    return dict(tokens=tokens, cotangent=cotangent, routes=routes, gate_weights=gate_weights, weight_gate=weight_gate, weight_up=weight_up, weight_down=weight_down)


def expert_pass(inputs, upstream, w_gate, w_up, w_down):
    gate_pre = jnp.dot(inputs, w_gate, preferred_element_type=jnp.float32)
    up_pre = jnp.dot(inputs, w_up, preferred_element_type=jnp.float32)
    sigmoid = jax.nn.sigmoid(gate_pre)
    swish = gate_pre * sigmoid
    hidden = (swish * up_pre).astype(jnp.bfloat16)
    output = jnp.dot(hidden, w_down, preferred_element_type=jnp.float32).astype(jnp.bfloat16)
    d_hidden = jnp.dot(upstream, w_down.T, preferred_element_type=jnp.float32)
    grad_down = jnp.dot(hidden.T, upstream, preferred_element_type=jnp.float32).astype(jnp.bfloat16)
    d_gate = (d_hidden * up_pre * sigmoid * (1.0 + gate_pre * (1.0 - sigmoid))).astype(jnp.bfloat16)
    d_up = (d_hidden * swish).astype(jnp.bfloat16)
    grad_gate = jnp.dot(inputs.T, d_gate, preferred_element_type=jnp.float32).astype(jnp.bfloat16)
    grad_up = jnp.dot(inputs.T, d_up, preferred_element_type=jnp.float32).astype(jnp.bfloat16)
    d_inputs = (jnp.dot(d_gate, w_gate.T, preferred_element_type=jnp.float32)
                + jnp.dot(d_up, w_up.T, preferred_element_type=jnp.float32)).astype(jnp.bfloat16)
    return output, d_inputs, grad_gate, grad_up, grad_down


def reference(tokens, cotangent, routes, gate_weights, weight_gate, weight_up, weight_down):
    choices_block = TOK_DEV * TOP
    flat_routes = routes.reshape(EXPERTS, choices_block).astype(jnp.int32)
    onehot = (flat_routes[:, :, None] == jnp.arange(EXPERTS, dtype=jnp.int32)[None, None, :]).astype(jnp.int32)
    position = jnp.sum((jnp.cumsum(onehot, axis=1) - onehot) * onehot, axis=2).astype(jnp.int32)
    block_ids = jnp.broadcast_to(jnp.arange(EXPERTS, dtype=jnp.int32)[:, None], (EXPERTS, choices_block))
    counter = jnp.arange(TOKENS * TOP, dtype=jnp.int32).reshape(EXPERTS, choices_block)
    token_ids = counter // TOP
    choice_ids = counter % TOP
    column = block_ids * CAP + position
    table_token = jnp.full((EXPERTS, EXPERTS * CAP), TOKENS, jnp.int32).at[flat_routes, column].set(token_ids)
    table_choice = jnp.zeros((EXPERTS, EXPERTS * CAP), jnp.int32).at[flat_routes, column].set(choice_ids)
    table_gate = jnp.zeros((EXPERTS, EXPERTS * CAP), jnp.float32).at[flat_routes, column].set(
        gate_weights.reshape(EXPERTS, choices_block).astype(jnp.float32))
    padded_tokens = jnp.concatenate([tokens, jnp.zeros((1, D), tokens.dtype)], axis=0)
    padded_cot = jnp.concatenate([cotangent, jnp.zeros((1, D), cotangent.dtype)], axis=0)

    def visit(carry, item):
        mixed_acc, dtok_acc, dgate_acc = carry
        index, choose, weight, w_gate, w_up, w_down = item
        inputs = padded_tokens[index]
        cot_rows = padded_cot[index].astype(jnp.float32)
        upstream = (weight[:, None] * cot_rows).astype(jnp.bfloat16)
        output, d_inputs, grad_gate, grad_up, grad_down = expert_pass(inputs, upstream, w_gate, w_up, w_down)
        out_wide = output.astype(jnp.float32)
        mixed_acc = mixed_acc.at[index].add(weight[:, None] * out_wide)
        dtok_acc = dtok_acc.at[index].add(d_inputs.astype(jnp.float32))
        dgate_acc = dgate_acc.at[index, choose].add(jnp.sum(out_wide * cot_rows, axis=1))
        return (mixed_acc, dtok_acc, dgate_acc), (grad_gate, grad_up, grad_down)

    start = (jnp.zeros((TOKENS + 1, D), jnp.float32), jnp.zeros((TOKENS + 1, D), jnp.float32),
             jnp.zeros((TOKENS + 1, TOP), jnp.float32))
    final, grads = lax.scan(visit, start, (table_token, table_choice, table_gate, weight_gate, weight_up, weight_down))
    mixed_acc, dtok_acc, dgate_acc = final
    return (mixed_acc[:TOKENS].astype(jnp.bfloat16), dtok_acc[:TOKENS].astype(jnp.bfloat16), dgate_acc[:TOKENS],
            grads[0], grads[1], grads[2])
```

```python
import functools

import jax
import jax.numpy as jnp
from jax import lax
from jax.experimental import pallas as pl
from jax.experimental.pallas import tpu as pltpu
from jax.sharding import PartitionSpec as P

MESH = pl.DeviceIdType.MESH
AXES = ("group", "ingroup")
PEERS = 128
CAP = 10
STRIDE = 37
UNSTRIDE = pow(STRIDE, -1, PEERS)
LANES = 128
VMEM_LIMIT = 56 * 1024 * 1024


def peer(j, sign):
    k = (j * STRIDE) % PEERS
    group, ingroup = lax.axis_index("group"), lax.axis_index("ingroup")
    core, z, x = ingroup % 2, (ingroup // 2) % 4, ingroup // 8
    dc, dz, dx, dy = k % 2, (k // 2) % 4, (k // 8) % 4, k // 32
    if sign < 0:
        dc, dz, dx, dy = 2 - dc, 4 - dz, 4 - dx, 4 - dy
    return (group + dy) % 4, (((x + dx) % 4) * 4 + (z + dz) % 4) * 2 + (core + dc) % 2


def relative(routes):
    group, ingroup = lax.axis_index("group"), lax.axis_index("ingroup")
    core, z, x = ingroup % 2, (ingroup // 2) % 4, ingroup // 8
    dy = (routes // 32 - group + 4) % 4
    dx = ((routes // 8) % 4 - x + 4) % 4
    dz = ((routes // 2) % 4 - z + 4) % 4
    dc = (routes % 2 - core + 2) % 2
    return ((dy * 32 + dx * 8 + dz * 2 + dc) * UNSTRIDE) % PEERS


def dispatch_kernel(source, gate, tokens, cotangent, x_in, u_in, x_out, u_out, x_send, u_send, x_recv, u_recv, own_sem):
    def one(j, carry):
        base = j * CAP
        for p in range(CAP):
            t = source[base + p]
            x_out[base + p] = tokens[t]
            u_out[base + p] = (gate[base + p] * cotangent[t].astype(jnp.float32)).astype(jnp.bfloat16)

        @pl.when(j > 0)
        def _():
            place = pl.ds(base, CAP)
            for src, dst, send, recv in ((x_out, x_in, x_send, x_recv), (u_out, u_in, u_send, u_recv)):
                pltpu.make_async_remote_copy(
                    src.at[place], dst.at[place], send, recv, device_id=peer(j, 1), device_id_type=MESH
                ).start()

        return carry

    lax.fori_loop(0, PEERS, one, 0)
    own = pl.ds(0, CAP)
    for src, dst in ((x_out, x_in), (u_out, u_in)):
        copy = pltpu.make_async_copy(src.at[own], dst.at[own], own_sem)
        copy.start()
        copy.wait()
    wait_all(x_out, x_in, x_send, x_recv)
    wait_all(u_out, u_in, u_send, u_recv)


def wait_all(src, dst, send, recv):
    others = pl.ds(CAP, (PEERS - 1) * CAP)
    every = pltpu.make_async_remote_copy(
        src.at[others], dst.at[others], send, recv,
        device_id=(lax.axis_index("group"), lax.axis_index("ingroup")), device_id_type=MESH,
    )
    every.wait_send()
    every.wait_recv()


def combine_kernel(slot, gate, out, grad, cotangent, mixed, grad_tokens, grad_gates, out_in, grad_in, o_send, g_send, o_recv, g_recv, own_sem):
    for src, dst, send, recv in ((out, out_in, o_send, o_recv), (grad, grad_in, g_send, g_recv)):
        def one(j, carry, src=src, dst=dst, send=send, recv=recv):
            place = pl.ds(j * CAP, CAP)
            pltpu.make_async_remote_copy(
                src.at[place], dst.at[place], send, recv, device_id=peer(j, -1), device_id_type=MESH
            ).start()
            return carry

        lax.fori_loop(1, PEERS, one, 0)
        own = pl.ds(0, CAP)
        copy = pltpu.make_async_copy(src.at[own], dst.at[own], own_sem)
        copy.start()
        copy.wait()
    tokens, choices = mixed.shape[0], grad_gates.shape[1]
    wait_all(out, out_in, o_send, o_recv)

    def mix(t, carry):
        cot = cotangent[t].astype(jnp.float32)
        total = jnp.zeros(cot.shape, jnp.float32)
        parts = []
        for k in range(choices):
            row = out_in[slot[t * choices + k]].astype(jnp.float32)
            total = total + gate[t * choices + k] * row
            parts.append(jnp.sum(row * cot, axis=0, keepdims=True))
        mixed[t] = total.astype(jnp.bfloat16)
        sums = jnp.sum(jnp.concatenate(parts, axis=0), axis=1, keepdims=True)
        grad_gates[t] = jnp.broadcast_to(sums, (choices, LANES))
        return carry

    lax.fori_loop(0, tokens, mix, 0)
    wait_all(grad, grad_in, g_send, g_recv)

    def add(t, carry):
        total = grad_in[slot[t * choices]].astype(jnp.float32)
        for k in range(1, choices):
            total = total + grad_in[slot[t * choices + k]].astype(jnp.float32)
        grad_tokens[t] = total.astype(jnp.bfloat16)
        return carry

    lax.fori_loop(0, tokens, add, 0)


def expert_pass(inputs, upstream, w_gate, w_up, w_down):
    gate_pre = jnp.dot(inputs, w_gate, preferred_element_type=jnp.float32)
    up_pre = jnp.dot(inputs, w_up, preferred_element_type=jnp.float32)
    sigmoid = jax.nn.sigmoid(gate_pre)
    swish = gate_pre * sigmoid
    hidden = (swish * up_pre).astype(jnp.bfloat16)
    output = jnp.dot(hidden, w_down, preferred_element_type=jnp.float32).astype(jnp.bfloat16)
    d_hidden = jnp.dot(upstream, w_down.T, preferred_element_type=jnp.float32)
    grad_down = jnp.dot(hidden.T, upstream, preferred_element_type=jnp.float32).astype(jnp.bfloat16)
    d_gate = (d_hidden * up_pre * sigmoid * (1.0 + gate_pre * (1.0 - sigmoid))).astype(jnp.bfloat16)
    d_up = (d_hidden * swish).astype(jnp.bfloat16)
    grad_gate = jnp.dot(inputs.T, d_gate, preferred_element_type=jnp.float32).astype(jnp.bfloat16)
    grad_up = jnp.dot(inputs.T, d_up, preferred_element_type=jnp.float32).astype(jnp.bfloat16)
    d_inputs = (
        jnp.dot(d_gate, w_gate.T, preferred_element_type=jnp.float32)
        + jnp.dot(d_up, w_up.T, preferred_element_type=jnp.float32)
    ).astype(jnp.bfloat16)
    return (output, d_inputs, grad_gate, grad_up, grad_down)


def plan(routes, gate_weights):
    order = relative(routes)
    onehot = order[:, :, None] == jnp.arange(PEERS, dtype=jnp.int32)[None, None, :]
    named = jnp.any(onehot, axis=1)
    weight = jnp.sum(jnp.where(onehot, gate_weights[:, :, None], 0.0), axis=1)
    count = routes.shape[0]
    lower = (jnp.arange(count)[:, None] >= jnp.arange(count)[None, :]).astype(jnp.bfloat16)
    upto = jnp.dot(lower, named.astype(jnp.bfloat16), preferred_element_type=jnp.float32).astype(jnp.int32)
    place = jnp.arange(CAP, dtype=jnp.int32)
    source = jnp.sum((upto[:, :, None] <= place).astype(jnp.int32), axis=0)
    taken = named[:, :, None] & (upto[:, :, None] - 1 == place)
    slot_gate = jnp.sum(jnp.where(taken, weight[:, :, None], 0.0), axis=0)
    position = jnp.sum(jnp.where(onehot, upto[:, None, :] - 1, 0), axis=2)
    return source.reshape(-1), slot_gate.reshape(-1), (order * CAP + position).reshape(-1)


def body(tokens, cotangent, routes, gate_weights, weight_gate, weight_up, weight_down):
    count, choices = routes.shape
    features = tokens.shape[1]
    tiles = features // LANES
    slots = PEERS * CAP
    source, slot_gate, slot = plan(routes, gate_weights)
    token_rows = jnp.pad(tokens.reshape(count, tiles, LANES), ((0, 8), (0, 0), (0, 0)))
    cot_rows = jnp.pad(cotangent.reshape(count, tiles, LANES), ((0, 8), (0, 0), (0, 0)))
    smem, vmem = pl.BlockSpec(memory_space=pltpu.SMEM), pl.BlockSpec(memory_space=pltpu.VMEM)
    hbm = pl.BlockSpec(memory_space=pl.ANY)
    slot_shape = jax.ShapeDtypeStruct((slots, tiles, LANES), jnp.bfloat16)
    semaphores = [pltpu.SemaphoreType.DMA] * 5
    x_in, u_in = pl.pallas_call(
        dispatch_kernel,
        out_shape=(slot_shape, slot_shape),
        in_specs=[smem, smem, vmem, vmem],
        out_specs=(hbm, hbm),
        scratch_shapes=[pltpu.VMEM(slot_shape.shape, jnp.bfloat16)] * 2 + semaphores,
        compiler_params=pltpu.CompilerParams(has_side_effects=True, vmem_limit_bytes=VMEM_LIMIT),
    )(source, slot_gate, token_rows, cot_rows)
    output, d_inputs, grad_gate, grad_up, grad_down = expert_pass(
        x_in.reshape(slots, features), u_in.reshape(slots, features), weight_gate[0], weight_up[0], weight_down[0]
    )
    row_shape = jax.ShapeDtypeStruct((count, tiles, LANES), jnp.bfloat16)
    mixed, grad_tokens, grad_gates = pl.pallas_call(
        combine_kernel,
        out_shape=(row_shape, row_shape, jax.ShapeDtypeStruct((count, choices, LANES), jnp.float32)),
        in_specs=[smem, smem, hbm, hbm, vmem],
        out_specs=(vmem, vmem, vmem),
        scratch_shapes=[pltpu.VMEM(slot_shape.shape, jnp.bfloat16)] * 2 + semaphores,
        compiler_params=pltpu.CompilerParams(has_side_effects=True, vmem_limit_bytes=VMEM_LIMIT),
    )(slot, gate_weights.reshape(-1), output.reshape(slot_shape.shape), d_inputs.reshape(slot_shape.shape), cot_rows)
    return (
        mixed.reshape(count, features),
        grad_tokens.reshape(count, features),
        grad_gates[:, :, 0],
        grad_gate[None],
        grad_up[None],
        grad_down[None],
    )


def solution(mesh):
    split2, split3 = P(AXES, None), P(AXES, None, None)
    return jax.shard_map(
        body,
        mesh=mesh,
        in_specs=(split2, split2, split2, split2, split3, split3, split3),
        out_specs=(split2, split2, split2, split3, split3, split3),
        check_vma=False,
    )
```

```python
import functools

import jax
import jax.numpy as jnp
from jax import lax
from jax.experimental import pallas as pl
from jax.experimental.pallas import tpu as pltpu
from jax.sharding import PartitionSpec as P

MESH = pl.DeviceIdType.MESH
AXES = ("group", "ingroup")
PEERS = 128
CAP = 10
STRIDE = 37
UNSTRIDE = pow(STRIDE, -1, PEERS)
LANES = 128
VMEM_LIMIT = 63 * 1024 * 1024
CHUNKS = 4
BLOCKS = PEERS // CHUNKS
ROWS = BLOCKS * CAP
GROUP = 16
WIDE = 256


def peer(j, sign):
    k = (j * STRIDE) % PEERS
    group, ingroup = lax.axis_index("group"), lax.axis_index("ingroup")
    core, z, x = ingroup % 2, (ingroup // 2) % 4, ingroup // 8
    dc, dz, dx, dy = k % 2, (k // 2) % 4, (k // 8) % 4, k // 32
    if sign < 0:
        dc, dz, dx, dy = 2 - dc, 4 - dz, 4 - dx, 4 - dy
    return (group + dy) % 4, (((x + dx) % 4) * 4 + (z + dz) % 4) * 2 + (core + dc) % 2


def relative(routes):
    group, ingroup = lax.axis_index("group"), lax.axis_index("ingroup")
    core, z, x = ingroup % 2, (ingroup // 2) % 4, ingroup // 8
    dy = (routes // 32 - group + 4) % 4
    dx = ((routes // 8) % 4 - x + 4) % 4
    dz = ((routes // 2) % 4 - z + 4) % 4
    dc = (routes % 2 - core + 2) % 2
    return ((dy * 32 + dx * 8 + dz * 2 + dc) * UNSTRIDE) % PEERS


def to_rows(native):
    tiles = native.shape[1] // LANES
    return jnp.swapaxes(jnp.stack([native[:, c * LANES : (c + 1) * LANES] for c in range(tiles)]), 0, 1)


def rows_to_native(rows, native, start):
    columns = jnp.swapaxes(rows, 0, 1)
    for c in range(columns.shape[0]):
        native[pl.ds(start, GROUP), c * LANES : (c + 1) * LANES] = columns[c]


def loop(count, step):
    def one(i, carry):
        step(i)
        return carry

    lax.fori_loop(0, count, one, 0)


def here():
    return (lax.axis_index("group"), lax.axis_index("ingroup"))


def wait_sent(block, sem):
    pltpu.make_async_remote_copy(block, block, sem, sem, device_id=here(), device_id_type=MESH).wait_send()


def wait_arrived(block, sem):
    pltpu.make_async_remote_copy(block, block, sem, sem, device_id=here(), device_id_type=MESH).wait_recv()


def dot(a, b, dims):
    return lax.dot_general(a, b, (dims, ((), ())), preferred_element_type=jnp.float32)


NN, NT, TN = ((1,), (0,)), ((1,), (1,)), ((0,), (0,))


def layer_kernel(
    source, slot_gate, slot, gate, tokens, cotangent, w_gate_hbm, w_up_hbm, w_down_hbm,
    mixed, grad_tokens, grad_gates, g_gate, g_up, g_down,
    token_rows, cot_rows, x_out, u_out, x_in, u_in, o_back, d_back, x, u, w_gate, w_up, w_down, hidden, d_pre, native,
    stage_pre, stage_down, sum_rows,
    w_sem, x_send, u_send, x_recv, u_recv, o_send, d_send, o_recv, d_recv, own_sem, stage_sem,
):
    weights = [
        pltpu.make_async_copy(src, dst, w_sem.at[i])
        for i, (src, dst) in enumerate(((w_gate_hbm, w_gate), (w_up_hbm, w_up), (w_down_hbm, w_down)))
    ]
    for copy in weights:
        copy.start()
    count, features = tokens.shape
    inner = hidden.shape[1]

    def spread(i):
        at = pl.ds(pl.multiple_of(i * GROUP, GROUP), GROUP)
        token_rows[at] = to_rows(tokens[at, :])
        cot_rows[at] = to_rows(cotangent[at, :])

    loop(count // GROUP, spread)
    token_rows[count] = jnp.zeros(token_rows.shape[1:], jnp.bfloat16)
    cot_rows[count] = jnp.zeros(cot_rows.shape[1:], jnp.bfloat16)

    def send(chunk):
        ring = lax.rem(chunk, 2)

        def one(b):
            base = b * CAP
            first = chunk * ROWS + base
            for p in range(CAP):
                t = source[first + p]
                x_out[ring, base + p] = token_rows[t]
                u_out[ring, base + p] = (slot_gate[first + p] * cot_rows[t].astype(jnp.float32)).astype(jnp.bfloat16)
            j = chunk * BLOCKS + b
            moves = ((x_out, x_in, x_send, x_recv), (u_out, u_in, u_send, u_recv))

            @pl.when(j > 0)
            def _():
                for src, dst, sent, arrived in moves:
                    pltpu.make_async_remote_copy(
                        src.at[ring, pl.ds(base, CAP)], dst.at[chunk, pl.ds(base, CAP)], sent.at[ring], arrived.at[chunk],
                        device_id=peer(j, 1), device_id_type=MESH,
                    ).start()

            @pl.when(j == 0)
            def _():
                for i, (src, dst, sent, arrived) in enumerate(moves):
                    copy = pltpu.make_async_copy(src.at[0, pl.ds(0, CAP)], dst.at[0, pl.ds(0, CAP)], own_sem.at[i])
                    copy.start()
                    copy.wait()

        loop(BLOCKS, one)

    def rest(ref, chunk, act):
        @pl.when(chunk == 0)
        def _():
            act(ref.at[0, pl.ds(CAP, ROWS - CAP)])

        @pl.when(chunk > 0)
        def _():
            act(ref.at[1, pl.ds(0, ROWS)])

    def give_back(src, dst, sent, arrived, chunk):
        def one(b):
            j = chunk * BLOCKS + b
            at = pl.ds(b * CAP, CAP)

            @pl.when(j > 0)
            def _():
                pltpu.make_async_remote_copy(
                    src.at[chunk, at], dst.at[chunk, at], sent.at[chunk], arrived.at[chunk],
                    device_id=peer(j, -1), device_id_type=MESH,
                ).start()

            @pl.when(j == 0)
            def _():
                copy = pltpu.make_async_copy(src.at[0, pl.ds(0, CAP)], dst.at[0, pl.ds(0, CAP)], own_sem.at[0])
                copy.start()
                copy.wait()

        loop(BLOCKS, one)

    def chunk_rows(chunk):
        return pl.ds(pl.multiple_of(chunk * ROWS, ROWS), ROWS)

    def work(chunk):
        for src, arrived, dst in ((x_in, x_recv, x), (u_in, u_recv, u)):
            rest(src, chunk, lambda block, arrived=arrived: wait_arrived(block, arrived.at[chunk]))

            def unpack(i, src=src, dst=dst):
                start = pl.multiple_of(i * GROUP, GROUP)
                rows_to_native(src[chunk, pl.ds(start, GROUP)], dst, pl.multiple_of(chunk * ROWS + start, GROUP))

            loop(ROWS // GROUP, unpack)
        at = chunk_rows(chunk)

        @pl.when(chunk == 0)
        def _():
            for copy in weights:
                copy.wait()

        def first(n):
            cols = pl.ds(pl.multiple_of(n * WIDE, WIDE), WIDE)
            gate_pre = dot(x[at, :], w_gate[:, cols], NN)
            up_pre = dot(x[at, :], w_up[:, cols], NN)
            sigmoid = jax.nn.sigmoid(gate_pre)
            swish = gate_pre * sigmoid
            hidden[at, cols] = (swish * up_pre).astype(jnp.bfloat16)
            d_hidden = dot(u[at, :], w_down[cols, :], NT)
            d_gate = d_hidden * up_pre * sigmoid * (1.0 + gate_pre * (1.0 - sigmoid))
            d_pre[at, cols] = d_gate.astype(jnp.bfloat16)
            d_pre[at, pl.ds(pl.multiple_of(inner + n * WIDE, WIDE), WIDE)] = (d_hidden * swish).astype(jnp.bfloat16)

        loop(inner // WIDE, first)

        def pack(dst):
            def one(i):
                rows = pl.ds(pl.multiple_of(i * GROUP, GROUP), GROUP)
                dst[chunk, rows] = to_rows(native[rows, :])

            loop(ROWS // GROUP, one)

        def output(n):
            cols = pl.ds(pl.multiple_of(n * WIDE, WIDE), WIDE)
            native[:, cols] = dot(hidden[at, :], w_down[:, cols], NN).astype(jnp.bfloat16)

        loop(features // WIDE, output)
        pack(x_in)
        give_back(x_in, o_back, o_send, o_recv, chunk)

        def backward(n):
            cols = pl.ds(pl.multiple_of(n * WIDE, WIDE), WIDE)
            native[:, cols] = (
                dot(d_pre[at, :inner], w_gate[cols, :], NT) + dot(d_pre[at, inner:], w_up[cols, :], NT)
            ).astype(jnp.bfloat16)

        loop(features // WIDE, backward)
        pack(u_in)

    send(0)
    send(1)

    def step(chunk):
        work(chunk)

        @pl.when(chunk < CHUNKS - 2)
        def _():
            rest(x_out, chunk, lambda block: wait_sent(block, x_send.at[lax.rem(chunk, 2)]))
            rest(u_out, chunk, lambda block: wait_sent(block, u_send.at[lax.rem(chunk, 2)]))
            send(chunk + 2)

    loop(CHUNKS, step)
    loop(CHUNKS, lambda chunk: give_back(u_in, d_back, d_send, d_recv, chunk))

    pre_tiles = features // WIDE

    def grad_pre(i):
        ring = lax.rem(i, 2)
        rows = pl.ds(pl.multiple_of(i * WIDE, WIDE), WIDE)
        copies = lambda: [
            pltpu.make_async_copy(stage_pre.at[ring, half], out.at[rows, :], stage_sem.at[ring, half])
            for half, out in enumerate((g_gate, g_up))
        ]

        @pl.when(i >= 2)
        def _():
            for copy in copies():
                copy.wait()

        for half in range(2):
            stage_pre[ring, half] = dot(x[:, rows], d_pre[:, half * inner : (half + 1) * inner], TN).astype(jnp.bfloat16)
        for copy in copies():
            copy.start()

    loop(pre_tiles, grad_pre)
    for ring in range(2):
        for half, out in enumerate((g_gate, g_up)):
            pltpu.make_async_copy(stage_pre.at[ring, half], out.at[pl.ds(0, WIDE), :], stage_sem.at[ring, half]).wait()

    half_features = features // 2

    def grad_down(i):
        rows = pl.ds(pl.multiple_of(i * WIDE, WIDE), WIDE)
        for half in range(2):
            cols = pl.ds(half * half_features, half_features)
            copy = pltpu.make_async_copy(stage_down.at[half], g_down.at[rows, cols], stage_sem.at[2, half])

            @pl.when(i >= 1)
            def _(copy=copy):
                copy.wait()

            stage_down[half] = dot(hidden[:, rows], u[:, cols], TN).astype(jnp.bfloat16)
            copy.start()

    loop(inner // WIDE, grad_down)
    for half in range(2):
        pltpu.make_async_copy(
            stage_down.at[half], g_down.at[pl.ds(0, WIDE), pl.ds(half * half_features, half_features)], stage_sem.at[2, half]
        ).wait()

    choices = grad_gates.shape[1]

    def wait_back(back, arrived):
        loop(CHUNKS, lambda chunk: rest(back, chunk, lambda block: wait_arrived(block, arrived.at[chunk])))

    def pick(back, t, k):
        s = slot[t * choices + k]
        return back[s // ROWS, lax.rem(s, ROWS)].astype(jnp.float32)

    wait_back(o_back, o_recv)

    def mix(i):
        def one(r):
            t = i * GROUP + r
            cot = cot_rows[t].astype(jnp.float32)
            total = jnp.zeros(cot.shape, jnp.float32)
            parts = []
            for k in range(choices):
                row = pick(o_back, t, k)
                total = total + gate[t * choices + k] * row
                parts.append(jnp.sum(row * cot, axis=0, keepdims=True))
            sum_rows[r] = total.astype(jnp.bfloat16)
            sums = jnp.sum(jnp.concatenate(parts, axis=0), axis=1, keepdims=True)
            grad_gates[t] = jnp.broadcast_to(sums, (choices, LANES))

        loop(GROUP, one)
        rows_to_native(sum_rows[...], mixed, pl.multiple_of(i * GROUP, GROUP))

    loop(count // GROUP, mix)
    wait_back(d_back, d_recv)

    def add(i):
        def one(r):
            t = i * GROUP + r
            total = pick(d_back, t, 0)
            for k in range(1, choices):
                total = total + pick(d_back, t, k)
            sum_rows[r] = total.astype(jnp.bfloat16)

        loop(GROUP, one)
        rows_to_native(sum_rows[...], grad_tokens, pl.multiple_of(i * GROUP, GROUP))

    loop(count // GROUP, add)

    for ref, sem in ((x_out, x_send), (u_out, u_send)):
        for ring in range(2):
            wait_sent(ref.at[ring], sem.at[ring])
    for ref, sem in ((x_in, o_send), (u_in, d_send)):
        loop(CHUNKS, lambda chunk, ref=ref, sem=sem: rest(ref, chunk, lambda block: wait_sent(block, sem.at[chunk])))


def plan(routes, gate_weights):
    order = relative(routes)
    onehot = order[:, :, None] == jnp.arange(PEERS, dtype=jnp.int32)[None, None, :]
    named = jnp.any(onehot, axis=1)
    weight = jnp.sum(jnp.where(onehot, gate_weights[:, :, None], 0.0), axis=1)
    count = routes.shape[0]
    lower = (jnp.arange(count)[:, None] >= jnp.arange(count)[None, :]).astype(jnp.bfloat16)
    upto = jnp.dot(lower, named.astype(jnp.bfloat16), preferred_element_type=jnp.float32).astype(jnp.int32)
    place = jnp.arange(CAP, dtype=jnp.int32)
    source = jnp.sum((upto[:, :, None] <= place).astype(jnp.int32), axis=0)
    taken = named[:, :, None] & (upto[:, :, None] - 1 == place)
    slot_gate = jnp.sum(jnp.where(taken, weight[:, :, None], 0.0), axis=0)
    position = jnp.sum(jnp.where(onehot, upto[:, None, :] - 1, 0), axis=2)
    return source.reshape(-1), slot_gate.reshape(-1), (order * CAP + position).reshape(-1)


def body(tokens, cotangent, routes, gate_weights, weight_gate, weight_up, weight_down):
    count, choices = routes.shape
    features, inner = weight_gate.shape[1:]
    tiles = features // LANES
    slots = PEERS * CAP
    source, slot_gate, slot = plan(routes, gate_weights)
    smem, vmem = pl.BlockSpec(memory_space=pltpu.SMEM), pl.BlockSpec(memory_space=pltpu.VMEM)
    hbm = pl.BlockSpec(memory_space=pl.ANY)
    bf16 = jnp.bfloat16
    semaphore = pltpu.SemaphoreType.DMA
    mixed, grad_tokens, grad_gates, grad_gate, grad_up, grad_down = pl.pallas_call(
        layer_kernel,
        out_shape=(
            jax.ShapeDtypeStruct(tokens.shape, bf16),
            jax.ShapeDtypeStruct(tokens.shape, bf16),
            jax.ShapeDtypeStruct((count, choices, LANES), jnp.float32),
            jax.ShapeDtypeStruct((features, inner), bf16),
            jax.ShapeDtypeStruct((features, inner), bf16),
            jax.ShapeDtypeStruct((inner, features), bf16),
        ),
        in_specs=[smem] * 4 + [vmem] * 2 + [hbm] * 3,
        out_specs=(vmem, vmem, vmem, hbm, hbm, hbm),
        scratch_shapes=[
            pltpu.VMEM((count + 8, tiles, LANES), bf16),
            pltpu.VMEM((count + 8, tiles, LANES), bf16),
            pltpu.VMEM((2, ROWS, tiles, LANES), bf16),
            pltpu.VMEM((2, ROWS, tiles, LANES), bf16),
            pltpu.VMEM((CHUNKS, ROWS, tiles, LANES), bf16),
            pltpu.VMEM((CHUNKS, ROWS, tiles, LANES), bf16),
            pltpu.VMEM((CHUNKS, ROWS, tiles, LANES), bf16),
            pltpu.VMEM((CHUNKS, ROWS, tiles, LANES), bf16),
            pltpu.VMEM((slots, features), bf16),
            pltpu.VMEM((slots, features), bf16),
            pltpu.VMEM((features, inner), bf16),
            pltpu.VMEM((features, inner), bf16),
            pltpu.VMEM((inner, features), bf16),
            pltpu.VMEM((slots, inner), bf16),
            pltpu.VMEM((slots, 2 * inner), bf16),
            pltpu.VMEM((ROWS, features), bf16),
            pltpu.VMEM((2, 2, WIDE, inner), bf16),
            pltpu.VMEM((2, WIDE, features // 2), bf16),
            pltpu.VMEM((GROUP, tiles, LANES), bf16),
            semaphore((3,)),
            semaphore((2,)),
            semaphore((2,)),
            semaphore((CHUNKS,)),
            semaphore((CHUNKS,)),
            semaphore((CHUNKS,)),
            semaphore((CHUNKS,)),
            semaphore((CHUNKS,)),
            semaphore((CHUNKS,)),
            semaphore((2,)),
            semaphore((3, 2)),
        ],
        compiler_params=pltpu.CompilerParams(has_side_effects=True, vmem_limit_bytes=VMEM_LIMIT),
        cost_estimate=pl.CostEstimate(
            flops=18 * slots * features * inner, bytes_accessed=12 * features * inner, transcendentals=slots * inner
        ),
    )(source, slot_gate, slot, gate_weights.reshape(-1), tokens, cotangent, weight_gate[0], weight_up[0], weight_down[0])
    return (mixed, grad_tokens, grad_gates[:, :, 0], grad_gate[None], grad_up[None], grad_down[None])


def solution(mesh):
    split2, split3 = P(AXES, None), P(AXES, None, None)
    return jax.shard_map(
        body,
        mesh=mesh,
        in_specs=(split2, split2, split2, split2, split3, split3, split3),
        out_specs=(split2, split2, split2, split3, split3, split3),
        check_vma=False,
    )
```

```python
import functools

import jax
import jax.numpy as jnp
from jax import lax
from jax.experimental import pallas as pl
from jax.experimental.pallas import tpu as pltpu
from jax.sharding import PartitionSpec as P

MESH = pl.DeviceIdType.MESH
AXES = ("group", "ingroup")
PEERS = 128
CAP = 10
STRIDE = 37
UNSTRIDE = pow(STRIDE, -1, PEERS)
LANES = 128
VMEM_LIMIT = 63 * 1024 * 1024
CHUNKS = 4
BLOCKS = PEERS // CHUNKS
ROWS = BLOCKS * CAP
GROUP = 16
WIDE = 256


def peer(j, sign):
    k = (j * STRIDE) % PEERS
    group, ingroup = lax.axis_index("group"), lax.axis_index("ingroup")
    core, z, x = ingroup % 2, (ingroup // 2) % 4, ingroup // 8
    dc, dz, dx, dy = k % 2, (k // 2) % 4, (k // 8) % 4, k // 32
    if sign < 0:
        dc, dz, dx, dy = 2 - dc, 4 - dz, 4 - dx, 4 - dy
    return (group + dy) % 4, (((x + dx) % 4) * 4 + (z + dz) % 4) * 2 + (core + dc) % 2


def relative(routes):
    group, ingroup = here()
    core, z, x = ingroup % 2, (ingroup // 2) % 4, ingroup // 8
    dy = (routes // 32 + (4 - group)) % 4
    dx = (routes // 8 + (4 - x)) % 4
    dz = (routes // 2 + (4 - z)) % 4
    dc = (routes + (2 - core)) % 2
    return ((dy * 32 + dx * 8 + dz * 2 + dc) * UNSTRIDE) % PEERS


def to_rows(native):
    tiles = native.shape[1] // LANES
    return jnp.swapaxes(jnp.stack([native[:, c * LANES : (c + 1) * LANES] for c in range(tiles)]), 0, 1)


def rows_to_native(rows, native, start):
    columns = jnp.swapaxes(rows, 0, 1)
    for c in range(columns.shape[0]):
        native[pl.ds(start, GROUP), c * LANES : (c + 1) * LANES] = columns[c]


def loop(count, step):
    def one(i, carry):
        step(i)
        return carry

    lax.fori_loop(0, count, one, 0)


def here():
    return (lax.axis_index("group"), lax.axis_index("ingroup"))


def wait_sent(block, sem):
    pltpu.make_async_remote_copy(block, block, sem, sem, device_id=here(), device_id_type=MESH).wait_send()


def wait_arrived(block, sem):
    pltpu.make_async_remote_copy(block, block, sem, sem, device_id=here(), device_id_type=MESH).wait_recv()


def greet():
    barrier = pltpu.get_barrier_semaphore()

    def one(j):
        pl.semaphore_signal(barrier, inc=1, device_id=peer(j + 1, 1), device_id_type=MESH)

    loop(PEERS - 1, one)


def dot(a, b, dims):
    return lax.dot_general(a, b, (dims, ((), ())), preferred_element_type=jnp.float32)


NN, NT, TN = ((1,), (0,)), ((1,), (1,)), ((0,), (0,))


def plan(routes, gates, source, weight, slot):
    choices, count = routes.shape
    order = relative(routes[...])
    peers = lax.broadcasted_iota(jnp.int32, (PEERS, count), 0)
    named = jnp.zeros((PEERS, count), jnp.float32)
    weights = jnp.zeros((PEERS, count), jnp.float32)
    for k in range(choices):
        same = order[k : k + 1, :] == peers
        named = jnp.where(same, 1.0, named)
        weights = jnp.where(same, gates[k : k + 1, :], weights)
    weight[...] = weights
    earlier = lax.broadcasted_iota(jnp.int32, (count, count), 0) <= lax.broadcasted_iota(jnp.int32, (count, count), 1)
    upto = dot(named.astype(jnp.bfloat16), jnp.where(earlier, 1.0, 0.0).astype(jnp.bfloat16), NN)
    ones = jnp.ones((8, count), jnp.bfloat16)
    for p in range(CAP):
        before = jnp.where(upto <= p, 1.0, 0.0).astype(jnp.bfloat16)
        source[p : p + 1, :] = jnp.clip(dot(ones, before, NT)[:1].astype(jnp.int32), 0, count)
    for k in range(choices):
        at = jnp.sum(jnp.where(order[k : k + 1, :] == peers, upto, 0.0), axis=0, keepdims=True)
        slot[k : k + 1, :] = jnp.clip(order[k : k + 1, :] * CAP + at.astype(jnp.int32) - 1, 0, PEERS * CAP - 1)


def layer_kernel(
    routes, gates, tokens, cotangent, w_gate_hbm, w_up_hbm, w_down_hbm,
    mixed, grad_tokens, grad_gates, g_gate, g_up, g_down, o_back,
    token_rows, cot_rows, x_out, u_out, x_in, u_in, d_back, x, u, w_gate, w_up, w_down, hidden, d_pre, native,
    stage_pre, stage_down, parts, source_v, weight_v, slot_v, source, weight, slot, gate,
    w_sem, x_send, u_send, x_recv, u_recv, o_send, d_send, o_recv, d_recv, own_sem, stage_sem, table_sem,
):
    greet()
    weights = [
        pltpu.make_async_copy(src, dst, w_sem.at[i])
        for i, (src, dst) in enumerate(((w_gate_hbm, w_gate), (w_up_hbm, w_up), (w_down_hbm, w_down)))
    ]
    for copy in weights:
        copy.start()
    count, features = tokens.shape
    inner = hidden.shape[1]
    plan(routes, gates, source_v, weight_v, slot_v)
    tables = [
        pltpu.make_async_copy(src, dst, table_sem.at[i])
        for i, (src, dst) in enumerate(((source_v, source), (weight_v, weight), (slot_v, slot), (gates, gate)))
    ]
    for copy in tables:
        copy.start()

    def spread(i):
        at = pl.ds(pl.multiple_of(i * GROUP, GROUP), GROUP)
        token_rows[at] = to_rows(tokens[at, :])
        cot_rows[at] = to_rows(cotangent[at, :])

    loop(count // GROUP, spread)
    token_rows[count] = jnp.zeros(token_rows.shape[1:], jnp.bfloat16)
    cot_rows[count] = jnp.zeros(cot_rows.shape[1:], jnp.bfloat16)

    for copy in tables:
        copy.wait()
    pl.semaphore_wait(pltpu.get_barrier_semaphore(), PEERS - 1)

    def send(fill, src, dst, sent, arrived):
        def one(j):
            chunk, b = j // BLOCKS, j % BLOCKS
            at = pl.ds(b * CAP, CAP)
            for p in range(CAP):
                src[chunk, b * CAP + p] = fill(source[p, j], j)

            @pl.when(j > 0)
            def _():
                pltpu.make_async_remote_copy(
                    src.at[chunk, at], dst.at[chunk, at], sent.at[chunk], arrived.at[chunk],
                    device_id=peer(j, 1), device_id_type=MESH,
                ).start()

            @pl.when(j == 0)
            def _():
                copy = pltpu.make_async_copy(src.at[0, pl.ds(0, CAP)], dst.at[0, pl.ds(0, CAP)], own_sem.at[0])
                copy.start()
                copy.wait()

        loop(PEERS, one)

    def scaled(t, j):
        return (weight[j, jnp.minimum(t, count - 1)] * cot_rows[t].astype(jnp.float32)).astype(jnp.bfloat16)

    send(lambda t, j: token_rows[t], x_out, x_in, x_send, x_recv)
    send(scaled, u_out, u_in, u_send, u_recv)

    def rest(ref, chunk, act):
        @pl.when(chunk == 0)
        def _():
            act(ref.at[0, pl.ds(CAP, ROWS - CAP)])

        @pl.when(chunk > 0)
        def _():
            act(ref.at[1, pl.ds(0, ROWS)])

    def give_back(src, dst, sent, arrived, chunk):
        def one(b):
            j = chunk * BLOCKS + b
            at = pl.ds(b * CAP, CAP)

            @pl.when(j > 0)
            def _():
                pltpu.make_async_remote_copy(
                    src.at[chunk, at], dst.at[chunk, at], sent.at[chunk], arrived.at[chunk],
                    device_id=peer(j, -1), device_id_type=MESH,
                ).start()

            @pl.when(j == 0)
            def _():
                copy = pltpu.make_async_copy(src.at[0, pl.ds(0, CAP)], dst.at[0, pl.ds(0, CAP)], own_sem.at[0])
                copy.start()
                copy.wait()

        loop(BLOCKS, one)

    def chunk_rows(chunk):
        return pl.ds(pl.multiple_of(chunk * ROWS, ROWS), ROWS)

    def take(src, arrived, dst, chunk):
        rest(src, chunk, lambda block: wait_arrived(block, arrived.at[chunk]))

        def unpack(i):
            start = pl.multiple_of(i * GROUP, GROUP)
            rows_to_native(src[chunk, pl.ds(start, GROUP)], dst, pl.multiple_of(chunk * ROWS + start, GROUP))

        loop(ROWS // GROUP, unpack)

    def pack(dst, chunk):
        def one(i):
            rows = pl.ds(pl.multiple_of(i * GROUP, GROUP), GROUP)
            dst[chunk, rows] = to_rows(native[rows, :])

        loop(ROWS // GROUP, one)

    def columns(n):
        return pl.ds(pl.multiple_of(n * WIDE, WIDE), WIDE)

    def forward(chunk):
        take(x_in, x_recv, x, chunk)
        at = chunk_rows(chunk)

        @pl.when(chunk == 0)
        def _():
            for copy in weights:
                copy.wait()

        def first(n):
            cols = columns(n)
            gate_pre = dot(x[at, :], w_gate[:, cols], NN)
            up_pre = dot(x[at, :], w_up[:, cols], NN)
            hidden[at, cols] = (gate_pre * jax.nn.sigmoid(gate_pre) * up_pre).astype(jnp.bfloat16)

        loop(inner // WIDE, first)

        def output(n):
            cols = columns(n)
            native[:, cols] = dot(hidden[at, :], w_down[:, cols], NN).astype(jnp.bfloat16)

        loop(features // WIDE, output)
        pack(x_in, chunk)
        give_back(x_in, o_back, o_send, o_recv, chunk)

    def backward(chunk):
        take(u_in, u_recv, u, chunk)
        at = chunk_rows(chunk)

        def first(n):
            cols = columns(n)
            gate_pre = dot(x[at, :], w_gate[:, cols], NN)
            up_pre = dot(x[at, :], w_up[:, cols], NN)
            sigmoid = jax.nn.sigmoid(gate_pre)
            d_hidden = dot(u[at, :], w_down[cols, :], NT)
            d_gate = d_hidden * up_pre * sigmoid * (1.0 + gate_pre * (1.0 - sigmoid))
            d_pre[at, cols] = d_gate.astype(jnp.bfloat16)
            d_up = d_hidden * (gate_pre * sigmoid)
            d_pre[at, pl.ds(pl.multiple_of(inner + n * WIDE, WIDE), WIDE)] = d_up.astype(jnp.bfloat16)

        loop(inner // WIDE, first)

        def second(n):
            cols = columns(n)
            native[:, cols] = (
                dot(d_pre[at, :inner], w_gate[cols, :], NT) + dot(d_pre[at, inner:], w_up[cols, :], NT)
            ).astype(jnp.bfloat16)

        loop(features // WIDE, second)
        pack(u_in, chunk)
        give_back(u_in, d_back, d_send, d_recv, chunk)

    loop(CHUNKS, forward)
    loop(CHUNKS, backward)

    pre_tiles = features // WIDE

    def grad_pre(i):
        ring = lax.rem(i, 2)
        rows = pl.ds(pl.multiple_of(i * WIDE, WIDE), WIDE)
        copies = lambda: [
            pltpu.make_async_copy(stage_pre.at[ring, half], out.at[rows, :], stage_sem.at[ring, half])
            for half, out in enumerate((g_gate, g_up))
        ]

        @pl.when(i >= 2)
        def _():
            for copy in copies():
                copy.wait()

        for half in range(2):
            stage_pre[ring, half] = dot(x[:, rows], d_pre[:, half * inner : (half + 1) * inner], TN).astype(jnp.bfloat16)
        for copy in copies():
            copy.start()

    loop(pre_tiles, grad_pre)
    for ring in range(2):
        for half, out in enumerate((g_gate, g_up)):
            pltpu.make_async_copy(stage_pre.at[ring, half], out.at[pl.ds(0, WIDE), :], stage_sem.at[ring, half]).wait()

    half_features = features // 2

    def grad_down(i):
        rows = pl.ds(pl.multiple_of(i * WIDE, WIDE), WIDE)
        for half in range(2):
            cols = pl.ds(half * half_features, half_features)
            copy = pltpu.make_async_copy(stage_down.at[half], g_down.at[rows, cols], stage_sem.at[2, half])

            @pl.when(i >= 1)
            def _(copy=copy):
                copy.wait()

            stage_down[half] = dot(hidden[:, rows], u[:, cols], TN).astype(jnp.bfloat16)
            copy.start()

    loop(inner // WIDE, grad_down)
    for half in range(2):
        pltpu.make_async_copy(
            stage_down.at[half], g_down.at[pl.ds(0, WIDE), pl.ds(half * half_features, half_features)], stage_sem.at[2, half]
        ).wait()

    choices = grad_gates.shape[0]

    def wait_back(back, arrived):
        loop(CHUNKS, lambda chunk: rest(back, chunk, lambda block: wait_arrived(block, arrived.at[chunk])))

    def pick(back, t, k):
        s = slot[k, t]
        return back[s // ROWS, lax.rem(s, ROWS)].astype(jnp.float32)

    wait_back(o_back, o_recv)
    loop(CHUNKS, lambda chunk: rest(x_out, chunk, lambda block: wait_sent(block, x_send.at[chunk])))
    landed = pltpu.make_async_copy(o_back, x_out, own_sem.at[1])
    landed.start()
    landed.wait()

    def mix(i):
        def one(r):
            t = i * GROUP + r
            cot = cot_rows[t].astype(jnp.float32)
            total = jnp.zeros(cot.shape, jnp.float32)
            for k in range(choices):
                row = pick(x_out, t, k)
                total = total + gate[k, t] * row
                parts[pl.ds(k * count + t, 1), :] = jnp.sum(row * cot, axis=0, keepdims=True)
            mixed[t] = total.astype(jnp.bfloat16)

        loop(GROUP, one)

    loop(count // GROUP, mix)
    for k in range(choices):
        grad_gates[k : k + 1, :] = jnp.sum(jnp.transpose(parts[k * count : (k + 1) * count, :]), axis=0, keepdims=True)
    wait_back(d_back, d_recv)

    def add(i):
        def one(r):
            t = i * GROUP + r
            total = pick(d_back, t, 0)
            for k in range(1, choices):
                total = total + pick(d_back, t, k)
            grad_tokens[t] = total.astype(jnp.bfloat16)

        loop(GROUP, one)

    loop(count // GROUP, add)

    for ref, sem in ((u_out, u_send), (x_in, o_send), (u_in, d_send)):
        loop(CHUNKS, lambda chunk, ref=ref, sem=sem: rest(ref, chunk, lambda block: wait_sent(block, sem.at[chunk])))


def body(tokens, cotangent, routes, gate_weights, weight_gate, weight_up, weight_down):
    count, choices = routes.shape
    features, inner = weight_gate.shape[1:]
    tiles = features // LANES
    slots = PEERS * CAP
    vmem = pl.BlockSpec(memory_space=pltpu.VMEM)
    hbm = pl.BlockSpec(memory_space=pl.ANY)
    bf16 = jnp.bfloat16
    semaphore = pltpu.SemaphoreType.DMA
    mixed, grad_tokens, grad_gates, grad_gate, grad_up, grad_down, _ = pl.pallas_call(
        layer_kernel,
        out_shape=(
            jax.ShapeDtypeStruct((count, tiles, LANES), bf16),
            jax.ShapeDtypeStruct((count, tiles, LANES), bf16),
            jax.ShapeDtypeStruct((choices, count), jnp.float32),
            jax.ShapeDtypeStruct((features, inner), bf16),
            jax.ShapeDtypeStruct((features, inner), bf16),
            jax.ShapeDtypeStruct((inner, features), bf16),
            jax.ShapeDtypeStruct((CHUNKS, ROWS, tiles, LANES), bf16),
        ),
        in_specs=[vmem] * 4 + [hbm] * 3,
        out_specs=(vmem, vmem, vmem, hbm, hbm, hbm, hbm),
        scratch_shapes=[
            pltpu.VMEM((count + 8, tiles, LANES), bf16),
            pltpu.VMEM((count + 8, tiles, LANES), bf16),
            pltpu.VMEM((CHUNKS, ROWS, tiles, LANES), bf16),
            pltpu.VMEM((CHUNKS, ROWS, tiles, LANES), bf16),
            pltpu.VMEM((CHUNKS, ROWS, tiles, LANES), bf16),
            pltpu.VMEM((CHUNKS, ROWS, tiles, LANES), bf16),
            pltpu.VMEM((CHUNKS, ROWS, tiles, LANES), bf16),
            pltpu.VMEM((slots, features), bf16),
            pltpu.VMEM((slots, features), bf16),
            pltpu.VMEM((features, inner), bf16),
            pltpu.VMEM((features, inner), bf16),
            pltpu.VMEM((inner, features), bf16),
            pltpu.VMEM((slots, inner), bf16),
            pltpu.VMEM((slots, 2 * inner), bf16),
            pltpu.VMEM((ROWS, features), bf16),
            pltpu.VMEM((2, 2, WIDE, inner), bf16),
            pltpu.VMEM((2, WIDE, features // 2), bf16),
            pltpu.VMEM((choices * count, LANES), jnp.float32),
            pltpu.VMEM((16, PEERS), jnp.int32),
            pltpu.VMEM((PEERS, count), jnp.float32),
            pltpu.VMEM((choices, count), jnp.int32),
            pltpu.SMEM((16, PEERS), jnp.int32),
            pltpu.SMEM((PEERS, count), jnp.float32),
            pltpu.SMEM((choices, count), jnp.int32),
            pltpu.SMEM((choices, count), jnp.float32),
            semaphore((3,)),
            semaphore((CHUNKS,)),
            semaphore((CHUNKS,)),
            semaphore((CHUNKS,)),
            semaphore((CHUNKS,)),
            semaphore((CHUNKS,)),
            semaphore((CHUNKS,)),
            semaphore((CHUNKS,)),
            semaphore((CHUNKS,)),
            semaphore((2,)),
            semaphore((3, 2)),
            semaphore((4,)),
        ],
        compiler_params=pltpu.CompilerParams(
            collective_id=0, has_side_effects=True, vmem_limit_bytes=VMEM_LIMIT
        ),
        cost_estimate=pl.CostEstimate(
            flops=18 * slots * features * inner, bytes_accessed=12 * features * inner, transcendentals=slots * inner
        ),
    )(routes.T, gate_weights.T, tokens, cotangent, weight_gate[0], weight_up[0], weight_down[0])
    return (mixed.reshape(tokens.shape), grad_tokens.reshape(tokens.shape), grad_gates.T, grad_gate[None], grad_up[None], grad_down[None])


def solution(mesh):
    split2, split3 = P(AXES, None), P(AXES, None, None)
    return jax.shard_map(
        body,
        mesh=mesh,
        in_specs=(split2, split2, split2, split2, split3, split3, split3),
        out_specs=(split2, split2, split2, split3, split3, split3),
        check_vma=False,
    )
```

```python
import functools

import jax
import jax.numpy as jnp
from jax import lax
from jax.experimental import pallas as pl
from jax.experimental.pallas import tpu as pltpu
from jax.sharding import PartitionSpec as P

MESH = pl.DeviceIdType.MESH
AXES = ("group", "ingroup")
PEERS = 128
CAP = 10
STRIDE = 37
UNSTRIDE = pow(STRIDE, -1, PEERS)
LANES = 128
VMEM_LIMIT = 63 * 1024 * 1024
CHUNKS = 4
BLOCKS = PEERS // CHUNKS
ROWS = BLOCKS * CAP
GROUP = 16
WIDE = 256
PIECES = 4


def peer(j, sign):
    k = (j * STRIDE) % PEERS
    group, ingroup = lax.axis_index("group"), lax.axis_index("ingroup")
    core, z, x = ingroup % 2, (ingroup // 2) % 4, ingroup // 8
    dc, dz, dx, dy = k % 2, (k // 2) % 4, (k // 8) % 4, k // 32
    if sign < 0:
        dc, dz, dx, dy = 2 - dc, 4 - dz, 4 - dx, 4 - dy
    return (group + dy) % 4, (((x + dx) % 4) * 4 + (z + dz) % 4) * 2 + (core + dc) % 2


def relative(routes):
    group, ingroup = here()
    core, z, x = ingroup % 2, (ingroup // 2) % 4, ingroup // 8
    dy = (routes // 32 + (4 - group)) % 4
    dx = (routes // 8 + (4 - x)) % 4
    dz = (routes // 2 + (4 - z)) % 4
    dc = (routes + (2 - core)) % 2
    return ((dy * 32 + dx * 8 + dz * 2 + dc) * UNSTRIDE) % PEERS


def to_rows(native):
    tiles = native.shape[1] // LANES
    return jnp.swapaxes(jnp.stack([native[:, c * LANES : (c + 1) * LANES] for c in range(tiles)]), 0, 1)


def rows_to_native(rows, native, start):
    columns = jnp.swapaxes(rows, 0, 1)
    for c in range(columns.shape[0]):
        native[pl.ds(start, GROUP), c * LANES : (c + 1) * LANES] = columns[c]


def loop(count, step):
    def one(i, carry):
        step(i)
        return carry

    lax.fori_loop(0, count, one, 0)


def here():
    return (lax.axis_index("group"), lax.axis_index("ingroup"))


def wait_sent(block, sem):
    pltpu.make_async_remote_copy(block, block, sem, sem, device_id=here(), device_id_type=MESH).wait_send()


def wait_arrived(block, sem):
    pltpu.make_async_remote_copy(block, block, sem, sem, device_id=here(), device_id_type=MESH).wait_recv()


def greet():
    barrier = pltpu.get_barrier_semaphore()

    def one(j):
        pl.semaphore_signal(barrier, inc=1, device_id=peer(j + 1, 1), device_id_type=MESH)

    loop(PEERS - 1, one)


def dot(a, b, dims):
    return lax.dot_general(a, b, (dims, ((), ())), preferred_element_type=jnp.float32)


NN, NT, TN = ((1,), (0,)), ((1,), (1,)), ((0,), (0,))


def plan(routes, gates, source, weight, slot):
    choices, count = routes.shape
    order = relative(routes[...])
    peers = lax.broadcasted_iota(jnp.int32, (PEERS, count), 0)
    named = jnp.zeros((PEERS, count), jnp.float32)
    weights = jnp.zeros((PEERS, count), jnp.float32)
    for k in range(choices):
        same = order[k : k + 1, :] == peers
        named = jnp.where(same, 1.0, named)
        weights = jnp.where(same, gates[k : k + 1, :], weights)
    weight[...] = weights
    earlier = lax.broadcasted_iota(jnp.int32, (count, count), 0) <= lax.broadcasted_iota(jnp.int32, (count, count), 1)
    upto = dot(named.astype(jnp.bfloat16), jnp.where(earlier, 1.0, 0.0).astype(jnp.bfloat16), NN)
    ones = jnp.ones((8, count), jnp.bfloat16)
    for p in range(CAP):
        before = jnp.where(upto <= p, 1.0, 0.0).astype(jnp.bfloat16)
        source[p : p + 1, :] = jnp.clip(dot(ones, before, NT)[:1].astype(jnp.int32), 0, count)
    for k in range(choices):
        at = jnp.sum(jnp.where(order[k : k + 1, :] == peers, upto, 0.0), axis=0, keepdims=True)
        slot[k : k + 1, :] = jnp.clip(order[k : k + 1, :] * CAP + at.astype(jnp.int32) - 1, 0, PEERS * CAP - 1)


def layer_kernel(
    routes, gates, tokens, cotangent, w_gate_hbm, w_up_hbm, w_down_hbm,
    mixed, grad_gates, slot_v, g_gate, g_up, g_down, o_back, d_back,
    token_rows, cot_rows, x_out, u_out, x_in, u_in, x, u, w_gate, w_up, w_down, hidden, d_pre, native,
    stage_pre, stage_down, parts, source_v, weight_v, source, weight, slot, gate,
    w_sem, x_send, u_send, x_recv, u_recv, o_send, d_send, o_recv, d_recv, own_sem, stage_sem, table_sem,
):
    greet()
    weights = [
        pltpu.make_async_copy(src, dst, w_sem.at[i])
        for i, (src, dst) in enumerate(((w_gate_hbm, w_gate), (w_up_hbm, w_up), (w_down_hbm, w_down)))
    ]
    for copy in weights:
        copy.start()
    count, features = tokens.shape
    inner = hidden.shape[1]
    plan(routes, gates, source_v, weight_v, slot_v)
    tables = [
        pltpu.make_async_copy(src, dst, table_sem.at[i])
        for i, (src, dst) in enumerate(((source_v, source), (weight_v, weight), (slot_v, slot), (gates, gate)))
    ]
    for copy in tables:
        copy.start()

    def spread(i):
        at = pl.ds(pl.multiple_of(i * GROUP, GROUP), GROUP)
        token_rows[at] = to_rows(tokens[at, :])
        cot_rows[at] = to_rows(cotangent[at, :])

    loop(count // GROUP, spread)
    token_rows[count] = jnp.zeros(token_rows.shape[1:], jnp.bfloat16)
    cot_rows[count] = jnp.zeros(cot_rows.shape[1:], jnp.bfloat16)

    for copy in tables:
        copy.wait()
    pl.semaphore_wait(pltpu.get_barrier_semaphore(), PEERS - 1)

    def block(j):
        return pl.ds(j * CAP, CAP)

    def move(src, dst, sent, arrived, j, sign):
        @pl.when(j > 0)
        def _():
            chunk = j // BLOCKS
            pltpu.make_async_remote_copy(
                src.at[block(j)], dst.at[block(j)], sent.at[chunk], arrived.at[chunk],
                device_id=peer(j, sign), device_id_type=MESH,
            ).start()

        @pl.when(j == 0)
        def _():
            copy = pltpu.make_async_copy(src.at[pl.ds(0, CAP)], dst.at[pl.ds(0, CAP)], own_sem.at[0])
            copy.start()
            copy.wait()

    def send(fill, src, dst, sent, arrived):
        def one(j):
            for p in range(CAP):
                src[j * CAP + p] = fill(source[p, j], j)
            move(src, dst, sent, arrived, j, 1)

        loop(PEERS, one)

    def scaled(t, j):
        return (weight[j, jnp.minimum(t, count - 1)] * cot_rows[t].astype(jnp.float32)).astype(jnp.bfloat16)

    send(lambda t, j: token_rows[t], x_out, x_in, x_send, x_recv)
    send(scaled, u_out, u_in, u_send, u_recv)

    def rest(ref, chunk, act):
        @pl.when(chunk == 0)
        def _():
            act(ref.at[pl.ds(CAP, ROWS - CAP)])

        @pl.when(chunk > 0)
        def _():
            act(ref.at[pl.ds(ROWS, ROWS)])

    def give_back(src, dst, sent, arrived, chunk):
        loop(BLOCKS, lambda b: move(src, dst, sent, arrived, chunk * BLOCKS + b, -1))

    def chunk_rows(chunk):
        return pl.ds(pl.multiple_of(chunk * ROWS, ROWS), ROWS)

    def take(src, arrived, dst, chunk):
        rest(src, chunk, lambda block: wait_arrived(block, arrived.at[chunk]))

        def unpack(i):
            start = pl.multiple_of(chunk * ROWS + i * GROUP, GROUP)
            rows_to_native(src[pl.ds(start, GROUP)], dst, start)

        loop(ROWS // GROUP, unpack)

    def pack(dst, chunk):
        def one(i):
            start = pl.multiple_of(i * GROUP, GROUP)
            dst[pl.ds(chunk * ROWS + start, GROUP)] = to_rows(native[pl.ds(start, GROUP), :])

        loop(ROWS // GROUP, one)

    def columns(n):
        return pl.ds(pl.multiple_of(n * WIDE, WIDE), WIDE)

    def forward(chunk):
        take(x_in, x_recv, x, chunk)
        at = chunk_rows(chunk)

        @pl.when(chunk == 0)
        def _():
            for copy in weights:
                copy.wait()

        def first(n):
            cols = columns(n)
            gate_pre = dot(x[at, :], w_gate[:, cols], NN)
            up_pre = dot(x[at, :], w_up[:, cols], NN)
            hidden[at, cols] = (gate_pre * jax.nn.sigmoid(gate_pre) * up_pre).astype(jnp.bfloat16)

        loop(inner // WIDE, first)

        def output(n):
            cols = columns(n)
            native[:, cols] = dot(hidden[at, :], w_down[:, cols], NN).astype(jnp.bfloat16)

        loop(features // WIDE, output)
        pack(x_in, chunk)
        give_back(x_in, o_back, o_send, o_recv, chunk)

    def backward(chunk):
        take(u_in, u_recv, u, chunk)
        at = chunk_rows(chunk)

        def first(n):
            cols = columns(n)
            gate_pre = dot(x[at, :], w_gate[:, cols], NN)
            up_pre = dot(x[at, :], w_up[:, cols], NN)
            sigmoid = jax.nn.sigmoid(gate_pre)
            d_hidden = dot(u[at, :], w_down[cols, :], NT)
            d_gate = d_hidden * up_pre * sigmoid * (1.0 + gate_pre * (1.0 - sigmoid))
            d_pre[at, cols] = d_gate.astype(jnp.bfloat16)
            d_up = d_hidden * (gate_pre * sigmoid)
            d_pre[at, pl.ds(pl.multiple_of(inner + n * WIDE, WIDE), WIDE)] = d_up.astype(jnp.bfloat16)

        loop(inner // WIDE, first)

        def second(n):
            cols = columns(n)
            native[:, cols] = (
                dot(d_pre[at, :inner], w_gate[cols, :], NT) + dot(d_pre[at, inner:], w_up[cols, :], NT)
            ).astype(jnp.bfloat16)

        loop(features // WIDE, second)
        pack(u_in, chunk)
        give_back(u_in, d_back, d_send, d_recv, chunk)

    loop(CHUNKS, forward)
    loop(CHUNKS, backward)

    pre_tiles = features // WIDE

    def grad_pre(i):
        ring = lax.rem(i, 2)
        rows = pl.ds(pl.multiple_of(i * WIDE, WIDE), WIDE)
        copies = lambda: [
            pltpu.make_async_copy(stage_pre.at[ring, half], out.at[rows, :], stage_sem.at[ring, half])
            for half, out in enumerate((g_gate, g_up))
        ]

        @pl.when(i >= 2)
        def _():
            for copy in copies():
                copy.wait()

        for half in range(2):
            stage_pre[ring, half] = dot(x[:, rows], d_pre[:, half * inner : (half + 1) * inner], TN).astype(jnp.bfloat16)
        for copy in copies():
            copy.start()

    loop(pre_tiles, grad_pre)
    for ring in range(2):
        for half, out in enumerate((g_gate, g_up)):
            pltpu.make_async_copy(stage_pre.at[ring, half], out.at[pl.ds(0, WIDE), :], stage_sem.at[ring, half]).wait()

    half_features = features // 2

    def grad_down(i):
        rows = pl.ds(pl.multiple_of(i * WIDE, WIDE), WIDE)
        for half in range(2):
            cols = pl.ds(half * half_features, half_features)
            copy = pltpu.make_async_copy(stage_down.at[half], g_down.at[rows, cols], stage_sem.at[2, half])

            @pl.when(i >= 1)
            def _(copy=copy):
                copy.wait()

            stage_down[half] = dot(hidden[:, rows], u[:, cols], TN).astype(jnp.bfloat16)
            copy.start()

    loop(inner // WIDE, grad_down)
    for half in range(2):
        pltpu.make_async_copy(
            stage_down.at[half], g_down.at[pl.ds(0, WIDE), pl.ds(half * half_features, half_features)], stage_sem.at[2, half]
        ).wait()

    choices = grad_gates.shape[0]

    def wait_back(back, arrived):
        loop(CHUNKS, lambda chunk: rest(back, chunk, lambda block: wait_arrived(block, arrived.at[chunk])))

    def pick(back, t, k):
        return back[slot[k, t]].astype(jnp.float32)

    wait_back(o_back, o_recv)
    loop(CHUNKS, lambda chunk: rest(x_out, chunk, lambda block: wait_sent(block, x_send.at[chunk])))
    landed = pltpu.make_async_copy(o_back, x_out, own_sem.at[1])
    landed.start()
    landed.wait()

    def mix(i):
        def one(r):
            t = i * GROUP + r
            cot = cot_rows[t].astype(jnp.float32)
            total = jnp.zeros(cot.shape, jnp.float32)
            for k in range(choices):
                row = pick(x_out, t, k)
                total = total + gate[k, t] * row
                parts[pl.ds(k * count + t, 1), :] = jnp.sum(row * cot, axis=0, keepdims=True)
            mixed[t] = total.astype(jnp.bfloat16)

        loop(GROUP, one)

    loop(count // GROUP, mix)
    for k in range(choices):
        grad_gates[k : k + 1, :] = jnp.sum(jnp.transpose(parts[k * count : (k + 1) * count, :]), axis=0, keepdims=True)
    wait_back(d_back, d_recv)

    for ref, sem in ((u_out, u_send), (x_in, o_send), (u_in, d_send)):
        loop(CHUNKS, lambda chunk, ref=ref, sem=sem: rest(ref, chunk, lambda block: wait_sent(block, sem.at[chunk])))


def finish_kernel(
    slot, d_back, mixed_rows, gates, g_gate, g_up, g_down, mixed, grad_tokens, grad_gates, out_gate, out_up, out_down,
    back, sums, hold_gate, hold_up, hold_down, back_sem, in_sem, out_sem,
):
    landed = pltpu.make_async_copy(d_back, back, back_sem)
    landed.start()
    loads, stores = [], []
    for i, (src, held, dst) in enumerate(
        ((g_gate, hold_gate, out_gate), (g_up, hold_up, out_up), (g_down, hold_down, out_down))
    ):
        part = src.shape[0] // PIECES
        for q in range(PIECES):
            at = pl.ds(q * part, part)
            loads.append(pltpu.make_async_copy(src.at[at], held.at[at], in_sem.at[i, q]))
            stores.append(pltpu.make_async_copy(held.at[at], dst.at[at], out_sem.at[i, q]))
    for copy in loads:
        copy.start()
    grad_gates[...] = gates[...]
    count, choices = mixed.shape[0], slot.shape[0]

    def spread(i):
        start = pl.multiple_of(i * GROUP, GROUP)
        rows_to_native(mixed_rows[pl.ds(start, GROUP)], mixed, start)

    loop(count // GROUP, spread)
    landed.wait()

    def add(i):
        start = pl.multiple_of(i * GROUP, GROUP)
        for r in range(GROUP):
            total = back[slot[0, start + r]].astype(jnp.float32)
            for k in range(1, choices):
                total = total + back[slot[k, start + r]].astype(jnp.float32)
            sums[r] = total.astype(jnp.bfloat16)
        rows_to_native(sums[...], grad_tokens, start)

    half = count // GROUP // 2
    loop(half, add)
    for load, store in zip(loads, stores):
        load.wait()
        store.start()
    loop(half, lambda i: add(half + i))
    for copy in stores:
        copy.wait()


def body(tokens, cotangent, routes, gate_weights, weight_gate, weight_up, weight_down):
    count, choices = routes.shape
    features, inner = weight_gate.shape[1:]
    tiles = features // LANES
    slots = PEERS * CAP
    vmem = pl.BlockSpec(memory_space=pltpu.VMEM)
    hbm = pl.BlockSpec(memory_space=pl.ANY)
    bf16 = jnp.bfloat16
    semaphore = pltpu.SemaphoreType.DMA
    weight_shapes = (
        jax.ShapeDtypeStruct((features, inner), bf16),
        jax.ShapeDtypeStruct((features, inner), bf16),
        jax.ShapeDtypeStruct((inner, features), bf16),
    )
    gates_shape = jax.ShapeDtypeStruct((choices, count), jnp.float32)
    slots_shape = jax.ShapeDtypeStruct((slots, tiles, LANES), bf16)
    mixed, grad_gates, slot, grad_gate, grad_up, grad_down, _, d_back = pl.pallas_call(
        layer_kernel,
        out_shape=(
            jax.ShapeDtypeStruct((count, tiles, LANES), bf16),
            gates_shape,
            jax.ShapeDtypeStruct((choices, count), jnp.int32),
            *weight_shapes,
            slots_shape,
            slots_shape,
        ),
        in_specs=[vmem] * 4 + [hbm] * 3,
        out_specs=(vmem, vmem, vmem, hbm, hbm, hbm, hbm, hbm),
        scratch_shapes=[
            pltpu.VMEM((count + 8, tiles, LANES), bf16),
            pltpu.VMEM((count + 8, tiles, LANES), bf16),
            pltpu.VMEM((slots, tiles, LANES), bf16),
            pltpu.VMEM((slots, tiles, LANES), bf16),
            pltpu.VMEM((slots, tiles, LANES), bf16),
            pltpu.VMEM((slots, tiles, LANES), bf16),
            pltpu.VMEM((slots, features), bf16),
            pltpu.VMEM((slots, features), bf16),
            pltpu.VMEM((features, inner), bf16),
            pltpu.VMEM((features, inner), bf16),
            pltpu.VMEM((inner, features), bf16),
            pltpu.VMEM((slots, inner), bf16),
            pltpu.VMEM((slots, 2 * inner), bf16),
            pltpu.VMEM((ROWS, features), bf16),
            pltpu.VMEM((2, 2, WIDE, inner), bf16),
            pltpu.VMEM((2, WIDE, features // 2), bf16),
            pltpu.VMEM((choices * count, LANES), jnp.float32),
            pltpu.VMEM((16, PEERS), jnp.int32),
            pltpu.VMEM((PEERS, count), jnp.float32),
            pltpu.SMEM((16, PEERS), jnp.int32),
            pltpu.SMEM((PEERS, count), jnp.float32),
            pltpu.SMEM((choices, count), jnp.int32),
            pltpu.SMEM((choices, count), jnp.float32),
            semaphore((3,)),
            semaphore((CHUNKS,)),
            semaphore((CHUNKS,)),
            semaphore((CHUNKS,)),
            semaphore((CHUNKS,)),
            semaphore((CHUNKS,)),
            semaphore((CHUNKS,)),
            semaphore((CHUNKS,)),
            semaphore((CHUNKS,)),
            semaphore((2,)),
            semaphore((3, 2)),
            semaphore((4,)),
        ],
        compiler_params=pltpu.CompilerParams(
            collective_id=0, has_side_effects=True, vmem_limit_bytes=VMEM_LIMIT
        ),
        cost_estimate=pl.CostEstimate(
            flops=18 * slots * features * inner, bytes_accessed=12 * features * inner, transcendentals=slots * inner
        ),
    )(routes.T, gate_weights.T, tokens, cotangent, weight_gate[0], weight_up[0], weight_down[0])
    smem = pl.BlockSpec(memory_space=pltpu.SMEM)
    mixed, grad_tokens, grad_gates, grad_gate, grad_up, grad_down = pl.pallas_call(
        finish_kernel,
        out_shape=(
            jax.ShapeDtypeStruct(tokens.shape, bf16),
            jax.ShapeDtypeStruct(tokens.shape, bf16),
            gates_shape,
            *weight_shapes,
        ),
        in_specs=[smem, hbm, vmem, vmem, hbm, hbm, hbm],
        out_specs=(vmem, vmem, vmem, hbm, hbm, hbm),
        scratch_shapes=[
            pltpu.VMEM((slots, tiles, LANES), bf16),
            pltpu.VMEM((GROUP, tiles, LANES), bf16),
            pltpu.VMEM((features, inner), bf16),
            pltpu.VMEM((features, inner), bf16),
            pltpu.VMEM((inner, features), bf16),
            semaphore,
            semaphore((3, PIECES)),
            semaphore((3, PIECES)),
        ],
        compiler_params=pltpu.CompilerParams(vmem_limit_bytes=VMEM_LIMIT),
        cost_estimate=pl.CostEstimate(flops=slots * features, bytes_accessed=12 * features * inner, transcendentals=0),
    )(slot, d_back, mixed, grad_gates, grad_gate, grad_up, grad_down)
    return (mixed, grad_tokens, grad_gates.T, grad_gate[None], grad_up[None], grad_down[None])


def solution(mesh):
    split2, split3 = P(AXES, None), P(AXES, None, None)
    return jax.shard_map(
        body,
        mesh=mesh,
        in_specs=(split2, split2, split2, split2, split3, split3, split3),
        out_specs=(split2, split2, split2, split3, split3, split3),
        check_vma=False,
    )
```

```python
import functools

import jax
import jax.numpy as jnp
from jax import lax
from jax.experimental import pallas as pl
from jax.experimental.pallas import tpu as pltpu
from jax.sharding import PartitionSpec as P

MESH = pl.DeviceIdType.MESH
AXES = ("group", "ingroup")
PEERS = 128
CAP = 10
STRIDE = 37
UNSTRIDE = pow(STRIDE, -1, PEERS)
LANES = 128
VMEM_LIMIT = 63 * 1024 * 1024
CHUNKS = 4
BLOCKS = PEERS // CHUNKS
ROWS = BLOCKS * CAP
GROUP = 16
WIDE = 256
PIECES = 4


def position():
    group, ingroup = here()
    return group, lax.div(ingroup, 8), lax.rem(lax.div(ingroup, 2), 4), lax.rem(ingroup, 2)


def peer(j, sign):
    k = lax.rem(j * STRIDE, PEERS)
    y, x, z, core = position()
    dy, dx, dz, dc = lax.div(k, 32), lax.rem(lax.div(k, 8), 4), lax.rem(lax.div(k, 2), 4), lax.rem(k, 2)
    if sign < 0:
        dy, dx, dz = 4 - dy, 4 - dx, 4 - dz
    return (lax.rem(y + dy, 4), (lax.rem(x + dx, 4) * 4 + lax.rem(z + dz, 4)) * 2 + lax.rem(core + dc, 2))


def relative(routes):
    group, x, z, core = position()
    dy = (routes // 32 + (4 - group)) % 4
    dx = (routes // 8 + (4 - x)) % 4
    dz = (routes // 2 + (4 - z)) % 4
    dc = (routes + (2 - core)) % 2
    return ((dy * 32 + dx * 8 + dz * 2 + dc) * UNSTRIDE) % PEERS


def to_rows(native):
    tiles = native.shape[1] // LANES
    return jnp.swapaxes(jnp.stack([native[:, c * LANES : (c + 1) * LANES] for c in range(tiles)]), 0, 1)


def rows_to_native(rows, native, start):
    columns = jnp.swapaxes(rows, 0, 1)
    for c in range(columns.shape[0]):
        native[pl.ds(start, GROUP), c * LANES : (c + 1) * LANES] = columns[c]


def loop(count, step):
    def one(i, carry):
        step(i)
        return carry

    lax.fori_loop(0, count, one, 0)


def here():
    return (lax.axis_index("group"), lax.axis_index("ingroup"))


def wait_sent(block, sem):
    pltpu.make_async_remote_copy(block, block, sem, sem, device_id=here(), device_id_type=MESH).wait_send()


def wait_arrived(block, sem):
    pltpu.make_async_remote_copy(block, block, sem, sem, device_id=here(), device_id_type=MESH).wait_recv()


def greet():
    barrier = pltpu.get_barrier_semaphore()
    y, x, z, core = position()
    ys = [lax.rem(y + d, 4) for d in range(4)]
    xs = [lax.rem(x + d, 4) * 8 for d in range(4)]
    zs = [lax.rem(z + d, 4) * 2 for d in range(4)]
    cores = [lax.rem(core + d, 2) for d in range(2)]
    planes = [[a + b for b in zs] for a in xs]
    for j in range(1, PEERS):
        k = (j * STRIDE) % PEERS
        device = (ys[k // 32], planes[(k // 8) % 4][(k // 2) % 4] + cores[k % 2])
        pl.semaphore_signal(barrier, inc=1, device_id=device, device_id_type=MESH)


def dot(a, b, dims):
    return lax.dot_general(a, b, (dims, ((), ())), preferred_element_type=jnp.float32)


NN, NT, TN = ((1,), (0,)), ((1,), (1,)), ((0,), (0,))


def plan(routes, gates, source, weight, slot):
    choices, count = routes.shape
    order = relative(routes[...])
    peers = lax.broadcasted_iota(jnp.int32, (PEERS, count), 0)
    named = jnp.zeros((PEERS, count), jnp.float32)
    weights = jnp.zeros((PEERS, count), jnp.float32)
    for k in range(choices):
        same = order[k : k + 1, :] == peers
        named = jnp.where(same, 1.0, named)
        weights = jnp.where(same, gates[k : k + 1, :], weights)
    weight[...] = weights
    earlier = lax.broadcasted_iota(jnp.int32, (count, count), 0) <= lax.broadcasted_iota(jnp.int32, (count, count), 1)
    upto = dot(named.astype(jnp.bfloat16), jnp.where(earlier, 1.0, 0.0).astype(jnp.bfloat16), NN)
    ones = jnp.ones((8, count), jnp.bfloat16)
    for p in range(CAP):
        before = jnp.where(upto <= p, 1.0, 0.0).astype(jnp.bfloat16)
        source[p : p + 1, :] = jnp.clip(dot(ones, before, NT)[:1].astype(jnp.int32), 0, count)
    for k in range(choices):
        at = jnp.sum(jnp.where(order[k : k + 1, :] == peers, upto, 0.0), axis=0, keepdims=True)
        slot[k : k + 1, :] = jnp.clip(order[k : k + 1, :] * CAP + at.astype(jnp.int32) - 1, 0, PEERS * CAP - 1)


def layer_kernel(
    routes, gates, tokens, cotangent, w_gate_hbm, w_up_hbm, w_down_hbm,
    mixed, grad_tokens, grad_gates, g_gate, g_up, g_down, o_back,
    token_rows, cot_rows, x_out, u_out, x_in, u_in, d_back, x, u, w_gate, w_up, w_down, hidden, d_pre, native,
    stage_pre, stage_down, parts, total, source_v, weight_v, slot_v, source, weight, slot, gate,
    w_sem, x_send, u_send, x_recv, u_recv, o_send, d_send, o_recv, d_recv, own_sem, stage_sem, table_sem,
):
    greet()
    weights = [
        pltpu.make_async_copy(src, dst, w_sem.at[i])
        for i, (src, dst) in enumerate(((w_gate_hbm, w_gate), (w_up_hbm, w_up), (w_down_hbm, w_down)))
    ]
    for copy in weights:
        copy.start()
    count, features = tokens.shape
    inner = hidden.shape[1]
    plan(routes, gates, source_v, weight_v, slot_v)
    tables = [
        pltpu.make_async_copy(src, dst, table_sem.at[i])
        for i, (src, dst) in enumerate(((source_v, source), (weight_v, weight), (slot_v, slot), (gates, gate)))
    ]
    for copy in tables:
        copy.start()

    def spread(i):
        at = pl.ds(pl.multiple_of(i * GROUP, GROUP), GROUP)
        token_rows[at] = to_rows(tokens[at, :])
        cot_rows[at] = to_rows(cotangent[at, :])

    loop(count // GROUP, spread)
    token_rows[count] = jnp.zeros(token_rows.shape[1:], jnp.bfloat16)
    cot_rows[count] = jnp.zeros(cot_rows.shape[1:], jnp.bfloat16)

    for copy in tables:
        copy.wait()
    pl.semaphore_wait(pltpu.get_barrier_semaphore(), PEERS - 1)

    def block(j):
        return pl.ds(j * CAP, CAP)

    def move(src, dst, sent, arrived, j, sign):
        @pl.when(j > 0)
        def _():
            chunk = lax.div(j, BLOCKS)
            pltpu.make_async_remote_copy(
                src.at[block(j)], dst.at[block(j)], sent.at[chunk], arrived.at[chunk],
                device_id=peer(j, sign), device_id_type=MESH,
            ).start()

        @pl.when(j == 0)
        def _():
            copy = pltpu.make_async_copy(src.at[pl.ds(0, CAP)], dst.at[pl.ds(0, CAP)], own_sem.at[0])
            copy.start()
            copy.wait()

    def send(fill, src, dst, sent, arrived):
        def one(j):
            for p in range(CAP):
                src[j * CAP + p] = fill(source[p, j], j)
            move(src, dst, sent, arrived, j, 1)

        loop(PEERS, one)

    def scaled(t, j):
        return (weight[j, jnp.minimum(t, count - 1)] * cot_rows[t].astype(jnp.float32)).astype(jnp.bfloat16)

    send(lambda t, j: token_rows[t], x_out, x_in, x_send, x_recv)
    send(scaled, u_out, u_in, u_send, u_recv)

    def rest(ref, chunk, act):
        @pl.when(chunk == 0)
        def _():
            act(ref.at[pl.ds(CAP, ROWS - CAP)])

        @pl.when(chunk > 0)
        def _():
            act(ref.at[pl.ds(ROWS, ROWS)])

    def give_back(src, dst, sent, arrived, chunk):
        loop(BLOCKS, lambda b: move(src, dst, sent, arrived, chunk * BLOCKS + b, -1))

    def chunk_rows(chunk):
        return pl.ds(pl.multiple_of(chunk * ROWS, ROWS), ROWS)

    def take(src, arrived, dst, chunk):
        rest(src, chunk, lambda block: wait_arrived(block, arrived.at[chunk]))

        def unpack(i):
            start = pl.multiple_of(chunk * ROWS + i * GROUP, GROUP)
            rows_to_native(src[pl.ds(start, GROUP)], dst, start)

        loop(ROWS // GROUP, unpack)

    def pack(dst, chunk):
        def one(i):
            start = pl.multiple_of(i * GROUP, GROUP)
            dst[pl.ds(chunk * ROWS + start, GROUP)] = to_rows(native[pl.ds(start, GROUP), :])

        loop(ROWS // GROUP, one)

    def columns(n):
        return pl.ds(pl.multiple_of(n * WIDE, WIDE), WIDE)

    def forward(chunk):
        take(x_in, x_recv, x, chunk)
        at = chunk_rows(chunk)

        @pl.when(chunk == 0)
        def _():
            for copy in weights:
                copy.wait()

        def first(n):
            cols = columns(n)
            gate_pre = dot(x[at, :], w_gate[:, cols], NN)
            up_pre = dot(x[at, :], w_up[:, cols], NN)
            hidden[at, cols] = (gate_pre * jax.nn.sigmoid(gate_pre) * up_pre).astype(jnp.bfloat16)

        loop(inner // WIDE, first)

        def output(n):
            cols = columns(n)
            native[:, cols] = dot(hidden[at, :], w_down[:, cols], NN).astype(jnp.bfloat16)

        loop(features // WIDE, output)
        pack(x_in, chunk)
        give_back(x_in, o_back, o_send, o_recv, chunk)

    def backward(chunk):
        take(u_in, u_recv, u, chunk)
        at = chunk_rows(chunk)

        def first(n):
            cols = columns(n)
            gate_pre = dot(x[at, :], w_gate[:, cols], NN)
            up_pre = dot(x[at, :], w_up[:, cols], NN)
            sigmoid = jax.nn.sigmoid(gate_pre)
            d_hidden = dot(u[at, :], w_down[cols, :], NT)
            d_gate = d_hidden * up_pre * sigmoid * (1.0 + gate_pre * (1.0 - sigmoid))
            d_pre[at, cols] = d_gate.astype(jnp.bfloat16)
            d_up = d_hidden * (gate_pre * sigmoid)
            d_pre[at, pl.ds(pl.multiple_of(inner + n * WIDE, WIDE), WIDE)] = d_up.astype(jnp.bfloat16)

        loop(inner // WIDE, first)

        def second(n):
            cols = columns(n)
            native[:, cols] = (
                dot(d_pre[at, :inner], w_gate[cols, :], NT) + dot(d_pre[at, inner:], w_up[cols, :], NT)
            ).astype(jnp.bfloat16)

        loop(features // WIDE, second)
        pack(u_in, chunk)
        give_back(u_in, d_back, d_send, d_recv, chunk)

    loop(CHUNKS, forward)
    loop(CHUNKS, backward)

    pre_tiles = features // WIDE

    def grad_pre(i):
        ring = lax.rem(i, 2)
        rows = pl.ds(pl.multiple_of(i * WIDE, WIDE), WIDE)
        copies = lambda: [
            pltpu.make_async_copy(stage_pre.at[ring, half], out.at[rows, :], stage_sem.at[ring, half])
            for half, out in enumerate((g_gate, g_up))
        ]

        @pl.when(i >= 2)
        def _():
            for copy in copies():
                copy.wait()

        for half in range(2):
            stage_pre[ring, half] = dot(x[:, rows], d_pre[:, half * inner : (half + 1) * inner], TN).astype(jnp.bfloat16)
        for copy in copies():
            copy.start()

    loop(pre_tiles, grad_pre)
    for ring in range(2):
        for half, out in enumerate((g_gate, g_up)):
            pltpu.make_async_copy(stage_pre.at[ring, half], out.at[pl.ds(0, WIDE), :], stage_sem.at[ring, half]).wait()

    half_features = features // 2

    def grad_down(i):
        rows = pl.ds(pl.multiple_of(i * WIDE, WIDE), WIDE)
        for half in range(2):
            cols = pl.ds(half * half_features, half_features)
            copy = pltpu.make_async_copy(stage_down.at[half], g_down.at[rows, cols], stage_sem.at[2, half])

            @pl.when(i >= 1)
            def _(copy=copy):
                copy.wait()

            stage_down[half] = dot(hidden[:, rows], u[:, cols], TN).astype(jnp.bfloat16)
            copy.start()

    loop(inner // WIDE, grad_down)
    for half in range(2):
        pltpu.make_async_copy(
            stage_down.at[half], g_down.at[pl.ds(0, WIDE), pl.ds(half * half_features, half_features)], stage_sem.at[2, half]
        ).wait()

    choices = grad_gates.shape[0]

    def wait_back(back, arrived):
        loop(CHUNKS, lambda chunk: rest(back, chunk, lambda block: wait_arrived(block, arrived.at[chunk])))

    def pick(back, t, k):
        return back[slot[k, t]].astype(jnp.float32)

    wait_back(o_back, o_recv)
    loop(CHUNKS, lambda chunk: rest(x_out, chunk, lambda block: wait_sent(block, x_send.at[chunk])))
    landed = pltpu.make_async_copy(o_back, x_out, own_sem.at[1])
    landed.start()
    landed.wait()

    def mix(i):
        def one(r):
            t = i * GROUP + r
            cot = cot_rows[t].astype(jnp.float32)
            total = jnp.zeros(cot.shape, jnp.float32)
            for k in range(choices):
                row = pick(x_out, t, k)
                total = total + gate[k, t] * row
                parts[pl.ds(k * count + t, 1), :] = jnp.sum(row * cot, axis=0, keepdims=True)
            mixed[t] = total.astype(jnp.bfloat16)

        loop(GROUP, one)

    loop(count // GROUP, mix)
    for k in range(choices):
        grad_gates[k : k + 1, :] = jnp.sum(jnp.transpose(parts[k * count : (k + 1) * count, :]), axis=0, keepdims=True)
    total[...] = jnp.zeros(total.shape, jnp.float32)

    def add(chunk):
        rest(d_back, chunk, lambda block: wait_arrived(block, d_recv.at[chunk]))

        def unpack(i):
            start = pl.multiple_of(i * GROUP, GROUP)
            rows_to_native(d_back[pl.ds(chunk * ROWS + start, GROUP)], native, start)

        loop(ROWS // GROUP, unpack)
        places = lax.broadcasted_iota(jnp.int32, (ROWS, count), 0) + chunk * ROWS
        owner = jnp.zeros((ROWS, count), jnp.float32)
        for k in range(choices):
            owner = jnp.where(places == slot_v[k : k + 1, :], 1.0, owner)
        owner = owner.astype(jnp.bfloat16)

        def block_sum(n):
            cols = columns(n)
            total[:, cols] += dot(owner, native[:, cols], TN)

        loop(features // WIDE, block_sum)

    loop(CHUNKS, add)
    grad_tokens[...] = total[...].astype(jnp.bfloat16)

    for ref, sem in ((u_out, u_send), (x_in, o_send), (u_in, d_send)):
        loop(CHUNKS, lambda chunk, ref=ref, sem=sem: rest(ref, chunk, lambda block: wait_sent(block, sem.at[chunk])))


def finish_kernel(
    mixed_rows, token_sums, gates, g_gate, g_up, g_down, mixed, grad_tokens, grad_gates, out_gate, out_up, out_down,
    hold_gate, hold_up, hold_down, in_sem, out_sem,
):
    loads, stores = [], []
    for i, (src, held, dst) in enumerate(
        ((g_gate, hold_gate, out_gate), (g_up, hold_up, out_up), (g_down, hold_down, out_down))
    ):
        part = src.shape[0] // PIECES
        for q in range(PIECES):
            at = pl.ds(q * part, part)
            loads.append(pltpu.make_async_copy(src.at[at], held.at[at], in_sem.at[i, q]))
            stores.append(pltpu.make_async_copy(held.at[at], dst.at[at], out_sem.at[i, q]))
    for copy in loads:
        copy.start()
    for load, store in zip(loads, stores):
        load.wait()
        store.start()
    grad_gates[...] = gates[...]
    grad_tokens[...] = token_sums[...]

    def spread(i):
        start = pl.multiple_of(i * GROUP, GROUP)
        rows_to_native(mixed_rows[pl.ds(start, GROUP)], mixed, start)

    loop(mixed.shape[0] // GROUP, spread)
    for copy in stores:
        copy.wait()


def body(tokens, cotangent, routes, gate_weights, weight_gate, weight_up, weight_down):
    count, choices = routes.shape
    features, inner = weight_gate.shape[1:]
    tiles = features // LANES
    slots = PEERS * CAP
    vmem = pl.BlockSpec(memory_space=pltpu.VMEM)
    hbm = pl.BlockSpec(memory_space=pl.ANY)
    bf16 = jnp.bfloat16
    semaphore = pltpu.SemaphoreType.DMA
    weight_shapes = (
        jax.ShapeDtypeStruct((features, inner), bf16),
        jax.ShapeDtypeStruct((features, inner), bf16),
        jax.ShapeDtypeStruct((inner, features), bf16),
    )
    gates_shape = jax.ShapeDtypeStruct((choices, count), jnp.float32)
    slots_shape = jax.ShapeDtypeStruct((slots, tiles, LANES), bf16)
    mixed, grad_tokens, grad_gates, grad_gate, grad_up, grad_down, _ = pl.pallas_call(
        layer_kernel,
        out_shape=(
            jax.ShapeDtypeStruct((count, tiles, LANES), bf16),
            jax.ShapeDtypeStruct(tokens.shape, bf16),
            gates_shape,
            *weight_shapes,
            slots_shape,
        ),
        in_specs=[vmem] * 4 + [hbm] * 3,
        out_specs=(vmem, vmem, vmem, hbm, hbm, hbm, hbm),
        scratch_shapes=[
            pltpu.VMEM((count + 8, tiles, LANES), bf16),
            pltpu.VMEM((count + 8, tiles, LANES), bf16),
            pltpu.VMEM((slots, tiles, LANES), bf16),
            pltpu.VMEM((slots, tiles, LANES), bf16),
            pltpu.VMEM((slots, tiles, LANES), bf16),
            pltpu.VMEM((slots, tiles, LANES), bf16),
            pltpu.VMEM((slots, tiles, LANES), bf16),
            pltpu.VMEM((slots, features), bf16),
            pltpu.VMEM((slots, features), bf16),
            pltpu.VMEM((features, inner), bf16),
            pltpu.VMEM((features, inner), bf16),
            pltpu.VMEM((inner, features), bf16),
            pltpu.VMEM((slots, inner), bf16),
            pltpu.VMEM((slots, 2 * inner), bf16),
            pltpu.VMEM((ROWS, features), bf16),
            pltpu.VMEM((2, 2, WIDE, inner), bf16),
            pltpu.VMEM((2, WIDE, features // 2), bf16),
            pltpu.VMEM((choices * count, LANES), jnp.float32),
            pltpu.VMEM((count, features), jnp.float32),
            pltpu.VMEM((16, PEERS), jnp.int32),
            pltpu.VMEM((PEERS, count), jnp.float32),
            pltpu.VMEM((choices, count), jnp.int32),
            pltpu.SMEM((16, PEERS), jnp.int32),
            pltpu.SMEM((PEERS, count), jnp.float32),
            pltpu.SMEM((choices, count), jnp.int32),
            pltpu.SMEM((choices, count), jnp.float32),
            semaphore((3,)),
            semaphore((CHUNKS,)),
            semaphore((CHUNKS,)),
            semaphore((CHUNKS,)),
            semaphore((CHUNKS,)),
            semaphore((CHUNKS,)),
            semaphore((CHUNKS,)),
            semaphore((CHUNKS,)),
            semaphore((CHUNKS,)),
            semaphore((2,)),
            semaphore((3, 2)),
            semaphore((4,)),
        ],
        compiler_params=pltpu.CompilerParams(
            collective_id=0, has_side_effects=True, vmem_limit_bytes=VMEM_LIMIT
        ),
        cost_estimate=pl.CostEstimate(
            flops=18 * slots * features * inner, bytes_accessed=12 * features * inner, transcendentals=slots * inner
        ),
    )(routes.T, gate_weights.T, tokens, cotangent, weight_gate[0], weight_up[0], weight_down[0])
    mixed, grad_tokens, grad_gates, grad_gate, grad_up, grad_down = pl.pallas_call(
        finish_kernel,
        out_shape=(
            jax.ShapeDtypeStruct(tokens.shape, bf16),
            jax.ShapeDtypeStruct(tokens.shape, bf16),
            gates_shape,
            *weight_shapes,
        ),
        in_specs=[vmem, vmem, vmem, hbm, hbm, hbm],
        out_specs=(vmem, vmem, vmem, hbm, hbm, hbm),
        scratch_shapes=[
            pltpu.VMEM((features, inner), bf16),
            pltpu.VMEM((features, inner), bf16),
            pltpu.VMEM((inner, features), bf16),
            semaphore((3, PIECES)),
            semaphore((3, PIECES)),
        ],
        compiler_params=pltpu.CompilerParams(vmem_limit_bytes=VMEM_LIMIT),
        cost_estimate=pl.CostEstimate(flops=slots * features, bytes_accessed=12 * features * inner, transcendentals=0),
    )(mixed, grad_tokens, grad_gates, grad_gate, grad_up, grad_down)
    return (mixed, grad_tokens, grad_gates.T, grad_gate[None], grad_up[None], grad_down[None])


def solution(mesh):
    split2, split3 = P(AXES, None), P(AXES, None, None)
    return jax.shard_map(
        body,
        mesh=mesh,
        in_specs=(split2, split2, split2, split2, split3, split3, split3),
        out_specs=(split2, split2, split2, split3, split3, split3),
        check_vma=False,
    )
```

```python
import functools

import jax
import jax.numpy as jnp
from jax import lax
from jax.experimental import pallas as pl
from jax.experimental.pallas import tpu as pltpu
from jax.sharding import PartitionSpec as P

MESH = pl.DeviceIdType.MESH
AXES = ("group", "ingroup")
PEERS = 128
CAP = 10
STRIDE = 37
UNSTRIDE = pow(STRIDE, -1, PEERS)
LANES = 128
VMEM_LIMIT = 63 * 1024 * 1024
CHUNKS = 4
BLOCKS = PEERS // CHUNKS
ROWS = BLOCKS * CAP
GROUP = 16
WIDE = 256
PIECES = 4


def position():
    group, ingroup = here()
    return group, lax.div(ingroup, 8), lax.rem(lax.div(ingroup, 2), 4), lax.rem(ingroup, 2)


def peer(j, sign):
    k = lax.rem(j * STRIDE, PEERS)
    y, x, z, core = position()
    dy, dx, dz, dc = lax.div(k, 32), lax.rem(lax.div(k, 8), 4), lax.rem(lax.div(k, 2), 4), lax.rem(k, 2)
    if sign < 0:
        dy, dx, dz = 4 - dy, 4 - dx, 4 - dz
    return (lax.rem(y + dy, 4), (lax.rem(x + dx, 4) * 4 + lax.rem(z + dz, 4)) * 2 + lax.rem(core + dc, 2))


def relative(routes):
    group, x, z, core = position()
    dy = (routes // 32 + (4 - group)) % 4
    dx = (routes // 8 + (4 - x)) % 4
    dz = (routes // 2 + (4 - z)) % 4
    dc = (routes + (2 - core)) % 2
    return ((dy * 32 + dx * 8 + dz * 2 + dc) * UNSTRIDE) % PEERS


def to_rows(native):
    tiles = native.shape[1] // LANES
    return jnp.swapaxes(jnp.stack([native[:, c * LANES : (c + 1) * LANES] for c in range(tiles)]), 0, 1)


def rows_to_native(rows, native, start):
    columns = jnp.swapaxes(rows, 0, 1)
    for c in range(columns.shape[0]):
        native[pl.ds(start, GROUP), c * LANES : (c + 1) * LANES] = columns[c]


def loop(count, step):
    def one(i, carry):
        step(i)
        return carry

    lax.fori_loop(0, count, one, 0)


def here():
    return (lax.axis_index("group"), lax.axis_index("ingroup"))


def wait_sent(block, sem):
    pltpu.make_async_remote_copy(block, block, sem, sem, device_id=here(), device_id_type=MESH).wait_send()


def wait_arrived(block, sem):
    pltpu.make_async_remote_copy(block, block, sem, sem, device_id=here(), device_id_type=MESH).wait_recv()


def greet():
    barrier = pltpu.get_barrier_semaphore()
    y, x, z, core = position()
    ys = [lax.rem(y + d, 4) for d in range(4)]
    xs = [lax.rem(x + d, 4) * 8 for d in range(4)]
    zs = [lax.rem(z + d, 4) * 2 for d in range(4)]
    cores = [lax.rem(core + d, 2) for d in range(2)]
    planes = [[a + b for b in zs] for a in xs]
    for j in range(1, PEERS):
        k = (j * STRIDE) % PEERS
        device = (ys[k // 32], planes[(k // 8) % 4][(k // 2) % 4] + cores[k % 2])
        pl.semaphore_signal(barrier, inc=1, device_id=device, device_id_type=MESH)


def dot(a, b, dims):
    return lax.dot_general(a, b, (dims, ((), ())), preferred_element_type=jnp.float32)


NN, NT, TN = ((1,), (0,)), ((1,), (1,)), ((0,), (0,))


def plan(routes, gates, source, weight, slot):
    choices, count = routes.shape
    order = relative(routes[...])
    peers = lax.broadcasted_iota(jnp.int32, (PEERS, count), 0)
    named = jnp.zeros((PEERS, count), jnp.float32)
    weights = jnp.zeros((PEERS, count), jnp.float32)
    for k in range(choices):
        same = order[k : k + 1, :] == peers
        named = jnp.where(same, 1.0, named)
        weights = jnp.where(same, gates[k : k + 1, :], weights)
    weight[...] = weights
    earlier = lax.broadcasted_iota(jnp.int32, (count, count), 0) <= lax.broadcasted_iota(jnp.int32, (count, count), 1)
    upto = dot(named.astype(jnp.bfloat16), jnp.where(earlier, 1.0, 0.0).astype(jnp.bfloat16), NN)
    ones = jnp.ones((8, count), jnp.bfloat16)
    for p in range(CAP):
        before = jnp.where(upto <= p, 1.0, 0.0).astype(jnp.bfloat16)
        source[p : p + 1, :] = jnp.clip(dot(ones, before, NT)[:1].astype(jnp.int32), 0, count)
    for k in range(choices):
        at = jnp.sum(jnp.where(order[k : k + 1, :] == peers, upto, 0.0), axis=0, keepdims=True)
        slot[k : k + 1, :] = jnp.clip(order[k : k + 1, :] * CAP + at.astype(jnp.int32) - 1, 0, PEERS * CAP - 1)


def layer_kernel(
    routes, gates, tokens, cotangent, w_gate_hbm, w_up_hbm, w_down_hbm,
    mixed, grad_tokens, grad_gates, g_gate, g_up, g_down, o_back,
    token_rows, cot_rows, x_out, u_out, x_in, u_in, d_back, x, u, w_gate, w_up, w_down, hidden, d_pre, native,
    stage_pre, stage_down, parts, total, source_v, weight_v, slot_v, source, weight, slot, gate,
    w_sem, x_send, u_send, x_recv, u_recv, o_send, d_send, o_recv, d_recv, own_sem, stage_sem, table_sem,
):
    greet()
    weights = [
        pltpu.make_async_copy(src, dst, w_sem.at[i])
        for i, (src, dst) in enumerate(((w_gate_hbm, w_gate), (w_up_hbm, w_up), (w_down_hbm, w_down)))
    ]
    for copy in weights:
        copy.start()
    count, features = tokens.shape
    inner = hidden.shape[1]
    plan(routes, gates, source_v, weight_v, slot_v)
    tables = [
        pltpu.make_async_copy(src, dst, table_sem.at[i])
        for i, (src, dst) in enumerate(((source_v, source), (weight_v, weight), (slot_v, slot), (gates, gate)))
    ]
    for copy in tables:
        copy.start()

    def spread(i):
        at = pl.ds(pl.multiple_of(i * GROUP, GROUP), GROUP)
        token_rows[at] = to_rows(tokens[at, :])
        cot_rows[at] = to_rows(cotangent[at, :])

    loop(count // GROUP, spread)
    token_rows[count] = jnp.zeros(token_rows.shape[1:], jnp.bfloat16)
    cot_rows[count] = jnp.zeros(cot_rows.shape[1:], jnp.bfloat16)

    for copy in tables:
        copy.wait()
    pl.semaphore_wait(pltpu.get_barrier_semaphore(), PEERS - 1)

    def block(j):
        return pl.ds(j * CAP, CAP)

    def move(src, dst, sent, arrived, j, sign):
        @pl.when(j > 0)
        def _():
            chunk = lax.div(j, BLOCKS)
            pltpu.make_async_remote_copy(
                src.at[block(j)], dst.at[block(j)], sent.at[chunk], arrived.at[chunk],
                device_id=peer(j, sign), device_id_type=MESH,
            ).start()

        @pl.when(j == 0)
        def _():
            copy = pltpu.make_async_copy(src.at[pl.ds(0, CAP)], dst.at[pl.ds(0, CAP)], own_sem.at[0])
            copy.start()
            copy.wait()

    def send(fill, src, dst, sent, arrived):
        def one(j):
            for p in range(CAP):
                src[j * CAP + p] = fill(source[p, j], j)
            move(src, dst, sent, arrived, j, 1)

        loop(PEERS, one)

    def scaled(t, j):
        return (weight[j, jnp.minimum(t, count - 1)] * cot_rows[t].astype(jnp.float32)).astype(jnp.bfloat16)

    send(lambda t, j: token_rows[t], x_out, x_in, x_send, x_recv)
    send(scaled, u_out, u_in, u_send, u_recv)

    def rest(ref, chunk, act):
        @pl.when(chunk == 0)
        def _():
            act(ref.at[pl.ds(CAP, ROWS - CAP)])

        @pl.when(chunk > 0)
        def _():
            act(ref.at[pl.ds(ROWS, ROWS)])

    def give_back(src, dst, sent, arrived, chunk):
        loop(BLOCKS, lambda b: move(src, dst, sent, arrived, chunk * BLOCKS + b, -1))

    def chunk_rows(chunk):
        return pl.ds(pl.multiple_of(chunk * ROWS, ROWS), ROWS)

    def take(src, arrived, dst, chunk):
        rest(src, chunk, lambda block: wait_arrived(block, arrived.at[chunk]))

        def unpack(i):
            start = pl.multiple_of(chunk * ROWS + i * GROUP, GROUP)
            rows_to_native(src[pl.ds(start, GROUP)], dst, start)

        loop(ROWS // GROUP, unpack)

    def pack(dst, chunk):
        def one(i):
            start = pl.multiple_of(i * GROUP, GROUP)
            dst[pl.ds(chunk * ROWS + start, GROUP)] = to_rows(native[pl.ds(start, GROUP), :])

        loop(ROWS // GROUP, one)

    def columns(n):
        return pl.ds(pl.multiple_of(n * WIDE, WIDE), WIDE)

    def forward(chunk):
        take(x_in, x_recv, x, chunk)
        at = chunk_rows(chunk)

        @pl.when(chunk == 0)
        def _():
            for copy in weights:
                copy.wait()

        def first(n):
            cols = columns(n)
            gate_pre = dot(x[at, :], w_gate[:, cols], NN)
            up_pre = dot(x[at, :], w_up[:, cols], NN)
            hidden[at, cols] = (gate_pre * jax.nn.sigmoid(gate_pre) * up_pre).astype(jnp.bfloat16)

        loop(inner // WIDE, first)

        def output(n):
            cols = columns(n)
            native[:, cols] = dot(hidden[at, :], w_down[:, cols], NN).astype(jnp.bfloat16)

        loop(features // WIDE, output)
        pack(x_in, chunk)
        give_back(x_in, o_back, o_send, o_recv, chunk)

    def backward(chunk):
        take(u_in, u_recv, u, chunk)
        at = chunk_rows(chunk)

        def first(n):
            cols = columns(n)
            gate_pre = dot(x[at, :], w_gate[:, cols], NN)
            up_pre = dot(x[at, :], w_up[:, cols], NN)
            sigmoid = jax.nn.sigmoid(gate_pre)
            d_hidden = dot(u[at, :], w_down[cols, :], NT)
            d_gate = d_hidden * up_pre * sigmoid * (1.0 + gate_pre * (1.0 - sigmoid))
            d_pre[at, cols] = d_gate.astype(jnp.bfloat16)
            d_up = d_hidden * (gate_pre * sigmoid)
            d_pre[at, pl.ds(pl.multiple_of(inner + n * WIDE, WIDE), WIDE)] = d_up.astype(jnp.bfloat16)

        loop(inner // WIDE, first)

        def second(n):
            cols = columns(n)
            native[:, cols] = (
                dot(d_pre[at, :inner], w_gate[cols, :], NT) + dot(d_pre[at, inner:], w_up[cols, :], NT)
            ).astype(jnp.bfloat16)

        loop(features // WIDE, second)
        pack(u_in, chunk)
        give_back(u_in, d_back, d_send, d_recv, chunk)

    loop(CHUNKS, forward)
    loop(CHUNKS, backward)

    pre_tiles = features // WIDE

    def grad_pre(i):
        ring = lax.rem(i, 2)
        rows = pl.ds(pl.multiple_of(i * WIDE, WIDE), WIDE)
        copies = lambda: [
            pltpu.make_async_copy(stage_pre.at[ring, half], out.at[rows, :], stage_sem.at[ring, half])
            for half, out in enumerate((g_gate, g_up))
        ]

        @pl.when(i >= 2)
        def _():
            for copy in copies():
                copy.wait()

        for half in range(2):
            stage_pre[ring, half] = dot(x[:, rows], d_pre[:, half * inner : (half + 1) * inner], TN).astype(jnp.bfloat16)
        for copy in copies():
            copy.start()

    loop(pre_tiles, grad_pre)
    for ring in range(2):
        for half, out in enumerate((g_gate, g_up)):
            pltpu.make_async_copy(stage_pre.at[ring, half], out.at[pl.ds(0, WIDE), :], stage_sem.at[ring, half]).wait()

    half_features = features // 2

    def grad_down(i):
        rows = pl.ds(pl.multiple_of(i * WIDE, WIDE), WIDE)
        for half in range(2):
            cols = pl.ds(half * half_features, half_features)
            copy = pltpu.make_async_copy(stage_down.at[half], g_down.at[rows, cols], stage_sem.at[2, half])

            @pl.when(i >= 1)
            def _(copy=copy):
                copy.wait()

            stage_down[half] = dot(hidden[:, rows], u[:, cols], TN).astype(jnp.bfloat16)
            copy.start()

    loop(inner // WIDE, grad_down)
    for half in range(2):
        pltpu.make_async_copy(
            stage_down.at[half], g_down.at[pl.ds(0, WIDE), pl.ds(half * half_features, half_features)], stage_sem.at[2, half]
        ).wait()

    choices = grad_gates.shape[0]

    def wait_back(back, arrived):
        loop(CHUNKS, lambda chunk: rest(back, chunk, lambda block: wait_arrived(block, arrived.at[chunk])))

    def pick(back, t, k):
        return back[slot[k, t]].astype(jnp.float32)

    wait_back(o_back, o_recv)
    loop(CHUNKS, lambda chunk: rest(x_out, chunk, lambda block: wait_sent(block, x_send.at[chunk])))
    landed = pltpu.make_async_copy(o_back, x_out, own_sem.at[1])
    landed.start()
    landed.wait()

    def mix(i):
        def one(r):
            t = i * GROUP + r
            cot = cot_rows[t].astype(jnp.float32)
            total = jnp.zeros(cot.shape, jnp.float32)
            for k in range(choices):
                row = pick(x_out, t, k)
                total = total + gate[k, t] * row
                parts[pl.ds(k * count + t, 1), :] = jnp.sum(row * cot, axis=0, keepdims=True)
            mixed[t] = total.astype(jnp.bfloat16)

        loop(GROUP, one)

    loop(count // GROUP, mix)
    for k in range(choices):
        grad_gates[k : k + 1, :] = jnp.sum(jnp.transpose(parts[k * count : (k + 1) * count, :]), axis=0, keepdims=True)
    total[...] = jnp.zeros(total.shape, jnp.float32)

    def add(chunk):
        rest(d_back, chunk, lambda block: wait_arrived(block, d_recv.at[chunk]))

        def unpack(i):
            start = pl.multiple_of(i * GROUP, GROUP)
            rows_to_native(d_back[pl.ds(chunk * ROWS + start, GROUP)], native, start)

        loop(ROWS // GROUP, unpack)
        places = lax.broadcasted_iota(jnp.int32, (ROWS, count), 0) + chunk * ROWS
        owner = jnp.zeros((ROWS, count), jnp.float32)
        for k in range(choices):
            owner = jnp.where(places == slot_v[k : k + 1, :], 1.0, owner)
        owner = owner.astype(jnp.bfloat16)

        def block_sum(n):
            cols = columns(n)
            total[:, cols] += dot(owner, native[:, cols], TN)

        loop(features // WIDE, block_sum)

    loop(CHUNKS, add)
    grad_tokens[...] = total[...].astype(jnp.bfloat16)

    for ref, sem in ((u_out, u_send), (x_in, o_send), (u_in, d_send)):
        loop(CHUNKS, lambda chunk, ref=ref, sem=sem: rest(ref, chunk, lambda block: wait_sent(block, sem.at[chunk])))


def finish_kernel(
    mixed_rows, token_sums, gates, g_gate, g_up, g_down, mixed, grad_tokens, grad_gates, out_gate, out_up, out_down,
    hold_gate, hold_up, hold_down, hold_sums, hold_rows, hold_mixed, in_sem, out_sem,
):
    loads, stores = [], []
    for i, (src, held, dst) in enumerate(
        ((g_gate, hold_gate, out_gate), (g_up, hold_up, out_up), (g_down, hold_down, out_down))
    ):
        part = src.shape[0] // PIECES
        for q in range(PIECES):
            at = pl.ds(q * part, part)
            loads.append(pltpu.make_async_copy(src.at[at], held.at[at], in_sem.at[i, q]))
            stores.append(pltpu.make_async_copy(held.at[at], dst.at[at], out_sem.at[i, q]))
    rows_in = pltpu.make_async_copy(mixed_rows, hold_rows, in_sem.at[3, 0])
    sums_in = pltpu.make_async_copy(token_sums, hold_sums, in_sem.at[3, 1])
    mixed_out = pltpu.make_async_copy(hold_mixed, mixed, out_sem.at[3, 0])
    sums_out = pltpu.make_async_copy(hold_sums, grad_tokens, out_sem.at[3, 1])
    for copy in (rows_in, sums_in, *loads):
        copy.start()
    grad_gates[...] = gates[...]
    rows_in.wait()

    def spread(i):
        start = pl.multiple_of(i * GROUP, GROUP)
        rows_to_native(hold_rows[pl.ds(start, GROUP)], hold_mixed, start)

    loop(hold_mixed.shape[0] // GROUP, spread)
    mixed_out.start()
    sums_in.wait()
    sums_out.start()
    for load, store in zip(loads, stores):
        load.wait()
        store.start()
    for copy in (mixed_out, sums_out, *stores):
        copy.wait()


def body(tokens, cotangent, routes, gate_weights, weight_gate, weight_up, weight_down):
    count, choices = routes.shape
    features, inner = weight_gate.shape[1:]
    tiles = features // LANES
    slots = PEERS * CAP
    vmem = pl.BlockSpec(memory_space=pltpu.VMEM)
    hbm = pl.BlockSpec(memory_space=pl.ANY)
    bf16 = jnp.bfloat16
    semaphore = pltpu.SemaphoreType.DMA
    weight_shapes = (
        jax.ShapeDtypeStruct((features, inner), bf16),
        jax.ShapeDtypeStruct((features, inner), bf16),
        jax.ShapeDtypeStruct((inner, features), bf16),
    )
    gates_shape = jax.ShapeDtypeStruct((choices, count), jnp.float32)
    slots_shape = jax.ShapeDtypeStruct((slots, tiles, LANES), bf16)
    mixed, grad_tokens, grad_gates, grad_gate, grad_up, grad_down, _ = pl.pallas_call(
        layer_kernel,
        out_shape=(
            jax.ShapeDtypeStruct((count, tiles, LANES), bf16),
            jax.ShapeDtypeStruct(tokens.shape, bf16),
            gates_shape,
            *weight_shapes,
            slots_shape,
        ),
        in_specs=[vmem] * 4 + [hbm] * 3,
        out_specs=(vmem, vmem, vmem, hbm, hbm, hbm, hbm),
        scratch_shapes=[
            pltpu.VMEM((count + 8, tiles, LANES), bf16),
            pltpu.VMEM((count + 8, tiles, LANES), bf16),
            pltpu.VMEM((slots, tiles, LANES), bf16),
            pltpu.VMEM((slots, tiles, LANES), bf16),
            pltpu.VMEM((slots, tiles, LANES), bf16),
            pltpu.VMEM((slots, tiles, LANES), bf16),
            pltpu.VMEM((slots, tiles, LANES), bf16),
            pltpu.VMEM((slots, features), bf16),
            pltpu.VMEM((slots, features), bf16),
            pltpu.VMEM((features, inner), bf16),
            pltpu.VMEM((features, inner), bf16),
            pltpu.VMEM((inner, features), bf16),
            pltpu.VMEM((slots, inner), bf16),
            pltpu.VMEM((slots, 2 * inner), bf16),
            pltpu.VMEM((ROWS, features), bf16),
            pltpu.VMEM((2, 2, WIDE, inner), bf16),
            pltpu.VMEM((2, WIDE, features // 2), bf16),
            pltpu.VMEM((choices * count, LANES), jnp.float32),
            pltpu.VMEM((count, features), jnp.float32),
            pltpu.VMEM((16, PEERS), jnp.int32),
            pltpu.VMEM((PEERS, count), jnp.float32),
            pltpu.VMEM((choices, count), jnp.int32),
            pltpu.SMEM((16, PEERS), jnp.int32),
            pltpu.SMEM((PEERS, count), jnp.float32),
            pltpu.SMEM((choices, count), jnp.int32),
            pltpu.SMEM((choices, count), jnp.float32),
            semaphore((3,)),
            semaphore((CHUNKS,)),
            semaphore((CHUNKS,)),
            semaphore((CHUNKS,)),
            semaphore((CHUNKS,)),
            semaphore((CHUNKS,)),
            semaphore((CHUNKS,)),
            semaphore((CHUNKS,)),
            semaphore((CHUNKS,)),
            semaphore((2,)),
            semaphore((3, 2)),
            semaphore((4,)),
        ],
        compiler_params=pltpu.CompilerParams(
            collective_id=0, has_side_effects=True, vmem_limit_bytes=VMEM_LIMIT
        ),
        cost_estimate=pl.CostEstimate(
            flops=18 * slots * features * inner, bytes_accessed=12 * features * inner, transcendentals=slots * inner
        ),
    )(routes.T, gate_weights.T, tokens, cotangent, weight_gate[0], weight_up[0], weight_down[0])
    mixed, grad_tokens, grad_gates, grad_gate, grad_up, grad_down = pl.pallas_call(
        finish_kernel,
        out_shape=(
            jax.ShapeDtypeStruct(tokens.shape, bf16),
            jax.ShapeDtypeStruct(tokens.shape, bf16),
            gates_shape,
            *weight_shapes,
        ),
        in_specs=[hbm, hbm, vmem, hbm, hbm, hbm],
        out_specs=(hbm, hbm, vmem, hbm, hbm, hbm),
        scratch_shapes=[
            pltpu.VMEM((features, inner), bf16),
            pltpu.VMEM((features, inner), bf16),
            pltpu.VMEM((inner, features), bf16),
            pltpu.VMEM(tokens.shape, bf16),
            pltpu.VMEM((count, tiles, LANES), bf16),
            pltpu.VMEM(tokens.shape, bf16),
            semaphore((4, PIECES)),
            semaphore((4, PIECES)),
        ],
        compiler_params=pltpu.CompilerParams(vmem_limit_bytes=VMEM_LIMIT),
        cost_estimate=pl.CostEstimate(flops=slots * features, bytes_accessed=12 * features * inner, transcendentals=0),
    )(mixed, grad_tokens, grad_gates, grad_gate, grad_up, grad_down)
    return (mixed, grad_tokens, grad_gates.T, grad_gate[None], grad_up[None], grad_down[None])


def solution(mesh):
    split2, split3 = P(AXES, None), P(AXES, None, None)
    return jax.shard_map(
        body,
        mesh=mesh,
        in_specs=(split2, split2, split2, split2, split3, split3, split3),
        out_specs=(split2, split2, split2, split3, split3, split3),
        check_vma=False,
    )
```
